256 devices in a mesh: row: 8 (over x, core), col: 32 (over z, y).
Axes of the slice: x: 4, y: 4, z: 8, core: 2. Of those that a mesh axis runs over, the one named last changes fastest.
Arguments:
- tangent: bfloat16 [32, 131072], P(None, ('col', 'row')), may hold values from -180 to 180
- activity: bfloat16 [131072], P(('col', 'row')), may hold values from -5 to 5
- block_keys: int32 [8, 512], P('row', 'col'), may hold values from 0 to 1073741823
Outputs:
- tangent_new: float32 [32, 131072], P(None, ('row', 'col'))
- next_state: float32 [131072], P(('row', 'col'))
- r_factor: float32 [32, 32], replicated
- first_factor: float32 [32, 32], replicated
The draws below stay inside these ranges and needn't reach their ends.
All inputs are finite; a program needn't handle non-finite values.
Results may differ from the reference program's by a relative error of at most 0.0006.
Values may be sent and summed in bfloat16 or wider, within the bound.
No kernel may reach another device: no remote copies, remote signals or barrier semaphores. Data moves between devices by JAX's collectives and lax.ppermute only.
A program may use at most 64 MiB of HBM per device.

```python
import math
import jax
import jax.numpy as jnp
from jax import lax

N = 131072
K = 32
KEYCOLS = 256
N_ROW = 8


def draw_tangent(key, part):
    key = jax.random.fold_in(key, 7)
    key_noise, key_scale, key_common = jax.random.split(key, 3)
    row_scales = jnp.exp(jax.random.uniform(key_scale, (K, 1), jnp.float32, 0.0, 3.0))
    common = jnp.clip(jax.random.normal(key_common, (1, N), jnp.float32), -4.0, 4.0)
    noise = jnp.clip(jax.random.normal(key_noise, (K, N), jnp.float32), -4.0, 4.0)
    vectors = row_scales * (common + 0.015 * noise)
    return vectors.astype(jnp.bfloat16)


def set_ends(entries, own_key, low, largest):
    index_at = [jax.random.randint(jax.random.fold_in(own_key, axis), (), 0, length) for axis, length in enumerate(entries.shape)]
    main_axis = entries.shape.index(max(entries.shape))
    next_to = index_at[:main_axis] + [(index_at[main_axis] + 1) % entries.shape[main_axis]] + index_at[main_axis + 1:]
    return entries.at[tuple(index_at)].set(low).at[tuple(next_to)].set(largest)


def level_of(rng, extent, pieces, smallest, high):
    level = 1.0
    for axis_at, parts in pieces:
        draws = jax.random.uniform(jax.random.fold_in(jax.random.fold_in(rng, 6), axis_at), (parts,), jnp.float32, smallest / len(pieces), high / len(pieces))
        level = level * jnp.repeat(jnp.exp(draws), extent[axis_at] // parts).reshape((-1,) + (1,) * (len(extent) - 1 - axis_at))
    return level


def bell_draw(rng, shape, deviation, reach, cuts=(), kind=jnp.bfloat16):
    entries = jax.random.normal(rng, shape, jnp.float32) * deviation
    if len(cuts) > 0:
        entries = level_of(rng, shape, cuts, -0.22, 0.18) * entries
    return jnp.clip(entries, min=-reach, max=reach).astype(kind)


def setup_inputs(seed: int = 0) -> dict:
    key_list = jax.random.split(jax.random.key(seed), 4)
    return {
        "tangent": draw_tangent(jax.random.fold_in(key_list[3], 71), 0),
        "activity": bell_draw(key_list[1], (N,), 1.0, 5.0, ((0, 256),)),
        "block_keys": set_ends(jax.random.randint(key_list[2], (N_ROW, N // KEYCOLS), 0, 1073741824), jax.random.fold_in(key_list[2], 1), 0, 1073741823).astype(jnp.int32),
    }


def coupling_values(tile_key, row_ids, column_ids):
    hashed = tile_key + row_ids * 374761393 + column_ids * 668265261
    hashed = hashed ^ lax.shift_right_logical(hashed, jnp.int32(15))
    hashed = hashed * 739982445
    hashed = hashed ^ lax.shift_right_logical(hashed, jnp.int32(13))
    hashed = hashed * 695872825
    hashed = hashed ^ lax.shift_right_logical(hashed, jnp.int32(16))
    return (jnp.bitwise_and(hashed, 255) - 128).astype(jnp.bfloat16)

def reference(tangent, activity, block_keys):
    vec_count = tangent.shape[0]
    stacked = jnp.concatenate([tangent, activity[None, :]], axis=0)
    span = min(512, N // N_ROW)
    group_rows = N // N_ROW
    column_ids = jnp.arange(N, dtype=jnp.int32)

    def one_block(block_index):
        first_row = block_index * span
        row_ids = first_row + jnp.arange(span, dtype=jnp.int32)
        keys_row = lax.dynamic_index_in_dim(block_keys, first_row // group_rows, 0, keepdims=False)
        key_columns = jnp.repeat(keys_row, KEYCOLS)
        block_tile = coupling_values(key_columns[None, :], row_ids[:, None], column_ids[None, :])
        return jnp.dot(block_tile.astype(jnp.float32), stacked.T.astype(jnp.float32), preferred_element_type=jnp.float32)
    drive = lax.map(one_block, jnp.arange(N // span, dtype=jnp.int32))
    drive = drive.reshape(N, vec_count + 1).T
    coupling_scale = 2.0 / math.sqrt(5461.25 * N)
    next_state = jnp.tanh(coupling_scale * drive[vec_count])
    grown = (coupling_scale * (1.0 - next_state * next_state))[None, :] * drive[:vec_count]
    hi = lax.Precision.HIGHEST
    gram_one = jnp.dot(grown, grown.T, precision=hi) / N
    lower_one = jnp.linalg.cholesky(gram_one)
    first = jax.scipy.linalg.solve_triangular(lower_one, grown, lower=True)
    gram_two = jnp.dot(first, first.T, precision=hi) / N
    lower_two = jnp.linalg.cholesky(gram_two)
    tangent_new = jax.scipy.linalg.solve_triangular(lower_two, first, lower=True)
    r_factor = jnp.dot(lower_one, lower_two, precision=hi).T
    return (tangent_new, next_state, r_factor, lower_one.T)
```

```python
import functools
import math

import jax
import jax.numpy as jnp
from jax import lax
from jax.experimental import pallas as pl
from jax.experimental.pallas import tpu as pltpu
from jax.sharding import Mesh
from jax.sharding import PartitionSpec as P

N = 131072
VECS = 32
PAD = 48
KEYCOLS = 256
X, CORE, Z, Y = 4, 2, 8, 4
OWN = N // (X * CORE * Z * Y)
ROWS = OWN * Y
SEG = OWN * X * CORE
GROUP = 32
SCALE = 2.0 / math.sqrt(5461.25 * N)
HIGH = lax.Precision.HIGHEST
VMEM_LIMIT = 48 * 2**20


def shift_right(value, amount):
    return lax.shift_right_logical(value, jnp.full(value.shape, amount, jnp.int32))


def coupling(value):
    value = value ^ shift_right(value, 15)
    value = value * jnp.int32(739982445)
    value = value ^ shift_right(value, 13)
    value = value * jnp.int32(695872825)
    value = value ^ shift_right(value, 16)
    return (value.astype(jnp.int8) ^ jnp.int8(-128)).astype(jnp.bfloat16)


def drive_kernel(rows_ref, bases_ref, vectors_ref, out_ref, *, segments, step):
    spread = lax.broadcasted_iota(jnp.int32, (GROUP, 128), 0) * jnp.int32(668265261)
    left = rows_ref[:, :128] + spread
    right = rows_ref[:, 128:] + spread
    groups = step * SEG // GROUP

    def body(number, total):
        first = pl.multiple_of(number * groups, groups)
        parts = []
        for group in range(groups):
            base = bases_ref[pl.ds(first + group, 1), :]
            parts.append(jnp.concatenate((coupling(base + left), coupling(base + right)), axis=1))
        vectors = jnp.concatenate([vectors_ref[number * step + k] for k in range(step)], axis=1)
        return total + jnp.dot(
            vectors, jnp.concatenate(parts, axis=0), preferred_element_type=jnp.float32
        )

    out_ref[...] = lax.fori_loop(
        0, segments // step, body, jnp.zeros(out_ref.shape, jnp.float32)
    )


def partial_drive(row_terms, bases, vectors, step):
    segments = vectors.shape[0]
    return pl.pallas_call(
        functools.partial(drive_kernel, segments=segments, step=step),
        grid=(row_terms.shape[1] // 256,),
        in_specs=[
            pl.BlockSpec((1, 256), lambda i: (0, i)),
            pl.BlockSpec(bases.shape, lambda i: (0, 0)),
            pl.BlockSpec(vectors.shape, lambda i: (0, 0, 0)),
        ],
        out_specs=pl.BlockSpec((PAD, 256), lambda i: (0, i)),
        out_shape=jax.ShapeDtypeStruct((PAD, row_terms.shape[1]), jnp.float32),
        compiler_params=pltpu.CompilerParams(vmem_limit_bytes=VMEM_LIMIT),
    )(row_terms, bases, vectors)


def pack_gram(gram):
    return jnp.concatenate([gram[8 * k : 8 * k + 8] for k in range(4)], axis=1)


def unpack_gram(packed):
    return jnp.concatenate([packed[:, 32 * k : 32 * k + 32] for k in range(4)], axis=0)


def gram_of(rows):
    return lax.dot_general(
        rows, rows, (((1,), (1,)), ((), ())), precision=HIGH, preferred_element_type=jnp.float32
    ) / N


def factor(gram):
    rows = lax.broadcasted_iota(jnp.int32, (VECS, VECS), 0)
    columns = lax.broadcasted_iota(jnp.int32, (VECS, VECS), 1)
    work = jnp.concatenate((gram, (rows == columns).astype(jnp.float32)), axis=1)
    row_at = lax.broadcasted_iota(jnp.int32, (VECS, 1), 0)
    scales = jnp.zeros((VECS, 1), jnp.float32)
    for j in range(VECS):
        pivot_row = work[j : j + 1, :]
        pivot = work[j : j + 1, j : j + 1]
        ratio = jnp.where(row_at > j, work[:, j : j + 1] / pivot, 0.0)
        scales = jnp.where(row_at == j, lax.rsqrt(pivot), scales)
        work = work - ratio * pivot_row
    work = work * scales
    upper = jnp.where(rows <= columns, work[:, :VECS], 0.0)
    return upper, work[:, VECS:]


def first_kernel(pieces_ref, state_ref, grown_ref, gram_ref):
    drive = pieces_ref[0] + pieces_ref[1] + pieces_ref[2] + pieces_ref[3]
    state = jnp.tanh(SCALE * drive[VECS : VECS + 1])
    grown = (SCALE * (1.0 - state * state)) * drive[:VECS]
    state_ref[...] = state
    grown_ref[...] = grown
    gram_ref[...] = pack_gram(gram_of(grown))


def second_kernel(grams_ref, grown_ref, first_ref, gram_ref, upper_ref):
    upper, inverse = factor(unpack_gram(jnp.sum(grams_ref[...], axis=0)))
    first = jnp.dot(inverse, grown_ref[...], precision=HIGH, preferred_element_type=jnp.float32)
    first_ref[...] = first
    upper_ref[...] = upper
    gram_ref[...] = pack_gram(gram_of(first))


def third_kernel(grams_ref, first_ref, upper_ref, result_ref, product_ref):
    upper, inverse = factor(unpack_gram(jnp.sum(grams_ref[...], axis=0)))
    result_ref[...] = jnp.dot(
        inverse, first_ref[...], precision=HIGH, preferred_element_type=jnp.float32
    )
    product_ref[...] = jnp.dot(
        upper, upper_ref[...], precision=HIGH, preferred_element_type=jnp.float32
    )


def spread_to(value, axes, count):
    return lax.all_to_all(jnp.broadcast_to(value, (count, *value.shape)), axes, 0, 0)


def gather_grams(gram):
    near = jnp.sum(spread_to(gram, ("x", "core"), X * CORE), axis=0)
    return spread_to(near, ("z", "y"), Z * Y)


def per_device(tangent, activity, block_keys):
    group = lax.axis_index("x") * CORE + lax.axis_index("core")
    z, y = lax.axis_index("z"), lax.axis_index("y")
    own = jnp.concatenate(
        (tangent, activity.reshape(1, -1), jnp.zeros((PAD - VECS - 1, OWN), jnp.bfloat16)), axis=0
    )
    vectors = lax.all_gather(own, ("x", "core"), axis=1, tiled=True)
    vectors = lax.all_gather(vectors, "z")
    keys = lax.all_gather(block_keys[0], "z")
    columns = (jnp.arange(Z, dtype=jnp.int32)[:, None] * Y + y) * SEG + jnp.arange(
        0, SEG, GROUP, dtype=jnp.int32
    )[None, :]
    bases = jnp.repeat(keys, KEYCOLS // GROUP, axis=1) + columns * 668265261
    bases = jnp.broadcast_to(bases.reshape(-1, 1), (bases.size, 128))
    row_ids = group * (N // (X * CORE)) + z * ROWS + jnp.arange(ROWS, dtype=jnp.int32)
    partial = partial_drive((row_ids * 374761393).reshape(1, ROWS), bases, vectors, 2)

    pieces = []
    for shift in range(Y):
        to = (y + shift) % Y
        piece = lax.dynamic_slice_in_dim(partial, to * OWN, OWN, 1)
        if shift:
            piece = lax.ppermute(piece, "y", [(i, (i + shift) % Y) for i in range(Y)])
        pieces.append(piece)

    state, grown, gram = pl.pallas_call(
        first_kernel,
        out_shape=(
            jax.ShapeDtypeStruct((1, OWN), jnp.float32),
            jax.ShapeDtypeStruct((VECS, OWN), jnp.float32),
            jax.ShapeDtypeStruct((8, 128), jnp.float32),
        ),
    )(jnp.stack(pieces))
    first, gram, upper = pl.pallas_call(
        second_kernel,
        out_shape=(
            jax.ShapeDtypeStruct((VECS, OWN), jnp.float32),
            jax.ShapeDtypeStruct((8, 128), jnp.float32),
            jax.ShapeDtypeStruct((VECS, VECS), jnp.float32),
        ),
    )(gather_grams(gram), grown)
    result, product = pl.pallas_call(
        third_kernel,
        out_shape=(
            jax.ShapeDtypeStruct((VECS, OWN), jnp.float32),
            jax.ShapeDtypeStruct((VECS, VECS), jnp.float32),
        ),
    )(gather_grams(gram), first, upper)
    return result, state.reshape(OWN), product, upper


def solution(mesh):
    split = Mesh(mesh.devices.reshape(X, CORE, Z, Y), ("x", "core", "z", "y"))
    columns, rows = ("z", "y", "x", "core"), ("x", "core", "z", "y")
    return jax.shard_map(
        per_device,
        mesh=split,
        in_specs=(P(None, columns), P(columns), P(("x", "core"), ("z", "y"))),
        out_specs=(P(None, rows), P(rows), P(), P()),
        check_vma=False,
    )
```

```python
import functools
import math

import jax
import jax.numpy as jnp
from jax import lax
from jax.experimental import pallas as pl
from jax.experimental.pallas import tpu as pltpu
from jax.sharding import Mesh
from jax.sharding import PartitionSpec as P

N = 131072
VECS = 32
PAD = 48
KEYCOLS = 256
X, CORE, Z, Y = 4, 2, 8, 4
OWN = N // (X * CORE * Z * Y)
ROWS = OWN * Y
SEG = OWN * X * CORE
GROUP = 32
LANES = 512
KEYS = SEG // KEYCOLS
SCALE = 2.0 / math.sqrt(5461.25 * N)
HIGH = lax.Precision.HIGHEST
VMEM_LIMIT = 48 * 2**20


def shift_right(value, amount):
    return lax.shift_right_logical(value, jnp.full(value.shape, amount, jnp.int32))


def coupling(value):
    value = value ^ shift_right(value, 15)
    value = value * jnp.int32(739982445)
    value = value ^ shift_right(value, 13)
    value = value * jnp.int32(695872825)
    value = value ^ shift_right(value, 16)
    return (value.astype(jnp.int8) ^ jnp.int8(-128)).astype(jnp.bfloat16)


def drive_kernel(places_ref, rows_ref, bases_ref, vectors_ref, *refs, segments):
    out_ref = refs[-1]
    spread = lax.broadcasted_iota(jnp.int32, (GROUP, 128), 0) * jnp.int32(668265261)
    starts = [rows_ref[:, 128 * k : 128 * k + 128] + spread for k in range(LANES // 128)]
    groups = SEG // GROUP

    def body(number, total):
        place = places_ref[number]
        first = pl.multiple_of(place * groups, groups)
        parts = []
        for group in range(groups):
            base = bases_ref[pl.ds(first + group, 1), :]
            parts.append(jnp.concatenate([coupling(base + start) for start in starts], axis=1))
        return total + jnp.dot(
            vectors_ref[place],
            jnp.concatenate(parts, axis=0),
            preferred_element_type=jnp.float32,
        )

    initial = refs[0][...] if len(refs) > 1 else jnp.zeros(out_ref.shape, jnp.float32)
    out_ref[...] = lax.fori_loop(0, segments, body, initial)


def partial_drive(places, row_terms, bases, vectors, earlier=()):
    segments = places.shape[0]
    lanes = pl.BlockSpec((PAD, LANES), lambda i: (0, i))
    hashes = segments * SEG * ROWS
    return pl.pallas_call(
        functools.partial(drive_kernel, segments=segments),
        grid=(ROWS // LANES,),
        in_specs=[
            pl.BlockSpec(memory_space=pltpu.SMEM),
            pl.BlockSpec((1, LANES), lambda i: (0, i)),
            pl.BlockSpec(bases.shape, lambda i: (0, 0)),
            pl.BlockSpec(vectors.shape, lambda i: (0, 0, 0)),
        ]
        + [lanes] * len(earlier),
        out_specs=lanes,
        out_shape=jax.ShapeDtypeStruct((PAD, ROWS), jnp.float32),
        cost_estimate=pl.CostEstimate(
            flops=hashes * 1500, bytes_accessed=vectors.size * 2, transcendentals=0
        ),
        compiler_params=pltpu.CompilerParams(vmem_limit_bytes=VMEM_LIMIT),
    )(places, row_terms, bases, vectors, *earlier)


def base_values(keys, places, y):
    columns = (places[:, None] * Y + y) * SEG + jnp.arange(0, SEG, GROUP, dtype=jnp.int32)[None, :]
    values = jnp.repeat(keys, KEYCOLS // GROUP, axis=1) + columns * 668265261
    return jnp.broadcast_to(values.reshape(-1, 1), (values.size, 128))


def pack_gram(gram):
    return jnp.concatenate([gram[8 * k : 8 * k + 8] for k in range(4)], axis=1)


def unpack_gram(packed):
    return jnp.concatenate([packed[:, 32 * k : 32 * k + 32] for k in range(4)], axis=0)


def gram_of(rows):
    return lax.dot_general(
        rows, rows, (((1,), (1,)), ((), ())), precision=HIGH, preferred_element_type=jnp.float32
    ) / N


def factor(gram):
    rows = lax.broadcasted_iota(jnp.int32, (VECS, VECS), 0)
    columns = lax.broadcasted_iota(jnp.int32, (VECS, VECS), 1)
    work = jnp.concatenate((gram, (rows == columns).astype(jnp.float32)), axis=1)
    row_at = lax.broadcasted_iota(jnp.int32, (VECS, 1), 0)
    scales = jnp.zeros((VECS, 1), jnp.float32)
    for j in range(VECS):
        pivot_row = work[j : j + 1, :]
        pivot = work[j : j + 1, j : j + 1]
        ratio = jnp.where(row_at > j, work[:, j : j + 1] / pivot, 0.0)
        scales = jnp.where(row_at == j, lax.rsqrt(pivot), scales)
        work = work - ratio * pivot_row
    work = work * scales
    upper = jnp.where(rows <= columns, work[:, :VECS], 0.0)
    return upper, work[:, VECS:]


def first_kernel(pieces_ref, state_ref, grown_ref, gram_ref):
    drive = pieces_ref[0] + pieces_ref[1] + pieces_ref[2] + pieces_ref[3]
    state = jnp.tanh(SCALE * drive[VECS : VECS + 1])
    grown = (SCALE * (1.0 - state * state)) * drive[:VECS]
    state_ref[...] = state
    grown_ref[...] = grown
    gram_ref[...] = pack_gram(gram_of(grown))


def second_kernel(grams_ref, grown_ref, first_ref, gram_ref, upper_ref):
    upper, inverse = factor(unpack_gram(jnp.sum(grams_ref[...], axis=0)))
    first = jnp.dot(inverse, grown_ref[...], precision=HIGH, preferred_element_type=jnp.float32)
    first_ref[...] = first
    upper_ref[...] = upper
    gram_ref[...] = pack_gram(gram_of(first))


def third_kernel(grams_ref, first_ref, upper_ref, result_ref, product_ref):
    upper, inverse = factor(unpack_gram(jnp.sum(grams_ref[...], axis=0)))
    result_ref[...] = jnp.dot(
        inverse, first_ref[...], precision=HIGH, preferred_element_type=jnp.float32
    )
    product_ref[...] = jnp.dot(
        upper, upper_ref[...], precision=HIGH, preferred_element_type=jnp.float32
    )


def spread_to(value, axes, count):
    return lax.all_to_all(jnp.broadcast_to(value, (count, *value.shape)), axes, 0, 0)


def gather_grams(gram):
    near = jnp.sum(spread_to(gram, ("x", "core"), X * CORE), axis=0)
    return spread_to(near, ("z", "y"), Z * Y)


def per_device(tangent, activity, block_keys):
    group = lax.axis_index("x") * CORE + lax.axis_index("core")
    z, y = lax.axis_index("z"), lax.axis_index("y")
    keys = block_keys[0]
    digits = [jnp.bitwise_and(shift_right(keys, 8 * k), 255).astype(jnp.bfloat16) for k in range(4)]
    digits = jnp.concatenate(digits + [jnp.zeros(OWN - 4 * KEYS, jnp.bfloat16)])
    own = jnp.concatenate(
        (
            tangent,
            activity.reshape(1, -1),
            digits.reshape(1, -1),
            jnp.zeros((PAD - VECS - 2, OWN), jnp.bfloat16),
        ),
        axis=0,
    )
    near = lax.all_gather(own, ("x", "core"), axis=1, tiled=True)
    vectors = lax.all_gather(near, "z")
    row_ids = group * (N // (X * CORE)) + z * ROWS + jnp.arange(ROWS, dtype=jnp.int32)
    row_terms = (row_ids * 374761393).reshape(1, ROWS)
    here = base_values(keys[None], z[None], y)
    partial = partial_drive(jnp.zeros(1, jnp.int32), row_terms, here, near[None])
    digits = lax.dynamic_slice(vectors, (0, VECS + 1, group * OWN), (Z, 1, 4 * KEYS))
    digits = digits.reshape(Z, 4, KEYS).astype(jnp.int32)
    keys = digits[:, 0] + digits[:, 1] * 256 + digits[:, 2] * 65536 + digits[:, 3] * 16777216
    bases = base_values(keys, jnp.arange(Z, dtype=jnp.int32), y)
    others = (z + jnp.arange(1, Z, dtype=jnp.int32)) % Z
    partial = partial_drive(others, row_terms, bases, vectors, (partial,))

    pieces = []
    for shift in range(Y):
        to = (y + shift) % Y
        piece = lax.dynamic_slice_in_dim(partial, to * OWN, OWN, 1)
        if shift:
            piece = lax.ppermute(piece, "y", [(i, (i + shift) % Y) for i in range(Y)])
        pieces.append(piece)

    state, grown, gram = pl.pallas_call(
        first_kernel,
        out_shape=(
            jax.ShapeDtypeStruct((1, OWN), jnp.float32),
            jax.ShapeDtypeStruct((VECS, OWN), jnp.float32),
            jax.ShapeDtypeStruct((8, 128), jnp.float32),
        ),
    )(jnp.stack(pieces))
    first, gram, upper = pl.pallas_call(
        second_kernel,
        out_shape=(
            jax.ShapeDtypeStruct((VECS, OWN), jnp.float32),
            jax.ShapeDtypeStruct((8, 128), jnp.float32),
            jax.ShapeDtypeStruct((VECS, VECS), jnp.float32),
        ),
    )(gather_grams(gram), grown)
    result, product = pl.pallas_call(
        third_kernel,
        out_shape=(
            jax.ShapeDtypeStruct((VECS, OWN), jnp.float32),
            jax.ShapeDtypeStruct((VECS, VECS), jnp.float32),
        ),
    )(gather_grams(gram), first, upper)
    return result, state.reshape(OWN), product, upper


def solution(mesh):
    split = Mesh(mesh.devices.reshape(X, CORE, Z, Y), ("x", "core", "z", "y"))
    columns, rows = ("z", "y", "x", "core"), ("x", "core", "z", "y")
    return jax.shard_map(
        per_device,
        mesh=split,
        in_specs=(P(None, columns), P(columns), P(("x", "core"), ("z", "y"))),
        out_specs=(P(None, rows), P(rows), P(), P()),
        check_vma=False,
    )
```

```python
import functools
import math

import jax
import jax.numpy as jnp
from jax import lax
from jax.experimental import pallas as pl
from jax.experimental.pallas import tpu as pltpu
from jax.sharding import Mesh
from jax.sharding import PartitionSpec as P

N = 131072
VECS = 32
PAD = 48
KEYCOLS = 256
X, CORE, Z, Y = 4, 2, 8, 4
OWN = N // (X * CORE * Z * Y)
ROWS = OWN * Y
SEG = OWN * X * CORE
GROUP = 32
GRAM_ROW = 40
LANES = 512
KEYS = SEG // KEYCOLS
SCALE = 2.0 / math.sqrt(5461.25 * N)
HIGH = lax.Precision.HIGHEST
VMEM_LIMIT = 48 * 2**20


def shift_right(value, amount):
    return lax.shift_right_logical(value, jnp.full(value.shape, amount, jnp.int32))


def coupling(value):
    value = value ^ shift_right(value, 15)
    value = value * jnp.int32(739982445)
    value = value ^ shift_right(value, 13)
    value = value * jnp.int32(695872825)
    value = value ^ shift_right(value, 16)
    return (value.astype(jnp.int8) ^ jnp.int8(-128)).astype(jnp.bfloat16)


def drive_kernel(places_ref, rows_ref, bases_ref, vectors_ref, *refs, segments):
    out_ref = refs[len(refs) // 2]
    spread = lax.broadcasted_iota(jnp.int32, (GROUP, 128), 0) * jnp.int32(668265261)
    starts = [rows_ref[:, 128 * k : 128 * k + 128] + spread for k in range(LANES // 128)]
    groups = SEG // GROUP

    def body(number, total):
        place = places_ref[number]
        first = pl.multiple_of(place * groups, groups)
        parts = []
        for group in range(groups):
            base = bases_ref[pl.ds(first + group, 1), :]
            parts.append(jnp.concatenate([coupling(base + start) for start in starts], axis=1))
        return total + jnp.dot(
            vectors_ref[place],
            jnp.concatenate(parts, axis=0),
            preferred_element_type=jnp.float32,
        )

    initial = refs[0][...] if len(refs) > 1 else jnp.zeros(out_ref.shape, jnp.float32)
    out_ref[...] = lax.fori_loop(0, segments, body, initial)
    if len(refs) > 1:
        gram_ref = refs[2]

        @pl.when(pl.program_id(0) == 0)
        def _():
            total = jnp.zeros((VECS, VECS), jnp.float32)
            for place in range(Z):
                own = vectors_ref[place][:VECS]
                total += lax.dot_general(
                    own, own, (((1,), (1,)), ((), ())), preferred_element_type=jnp.float32
                )
            gram_ref[...] = pack_gram(total / N)

        out_ref[GRAM_ROW:, :128] = gram_ref[...]


def partial_drive(places, row_terms, bases, vectors, earlier=()):
    segments = places.shape[0]
    lanes = pl.BlockSpec((PAD, LANES), lambda i: (0, i))
    hashes = segments * SEG * ROWS
    return pl.pallas_call(
        functools.partial(drive_kernel, segments=segments),
        grid=(ROWS // LANES,),
        in_specs=[
            pl.BlockSpec(memory_space=pltpu.SMEM),
            pl.BlockSpec((1, LANES), lambda i: (0, i)),
            pl.BlockSpec(bases.shape, lambda i: (0, 0)),
            pl.BlockSpec(vectors.shape, lambda i: (0, 0, 0)),
        ]
        + [lanes] * len(earlier),
        out_specs=lanes,
        out_shape=jax.ShapeDtypeStruct((PAD, ROWS), jnp.float32),
        scratch_shapes=[pltpu.VMEM((8, 128), jnp.float32)] * len(earlier),
        cost_estimate=pl.CostEstimate(
            flops=hashes * 1500, bytes_accessed=vectors.size * 2, transcendentals=0
        ),
        compiler_params=pltpu.CompilerParams(vmem_limit_bytes=VMEM_LIMIT),
    )(places, row_terms, bases, vectors, *earlier)


def base_values(keys, places, y):
    columns = (places[:, None] * Y + y) * SEG + jnp.arange(0, SEG, GROUP, dtype=jnp.int32)[None, :]
    values = jnp.repeat(keys, KEYCOLS // GROUP, axis=1) + columns * 668265261
    return jnp.broadcast_to(values.reshape(-1, 1), (values.size, 128))


def pack_gram(gram):
    return jnp.concatenate([gram[8 * k : 8 * k + 8] for k in range(4)], axis=1)


def unpack_gram(packed):
    return jnp.concatenate([packed[:, 32 * k : 32 * k + 32] for k in range(4)], axis=0)


def gram_of(rows):
    return lax.dot_general(
        rows, rows, (((1,), (1,)), ((), ())), precision=HIGH, preferred_element_type=jnp.float32
    ) / N


def dot(left, right):
    return jnp.dot(left, right, precision=HIGH, preferred_element_type=jnp.float32)


def factor(gram, floor=0.0):
    rows = lax.broadcasted_iota(jnp.int32, (VECS, VECS), 0)
    columns = lax.broadcasted_iota(jnp.int32, (VECS, VECS), 1)
    work = jnp.concatenate((gram, (rows == columns).astype(jnp.float32)), axis=1)
    row_at = lax.broadcasted_iota(jnp.int32, (VECS, 1), 0)
    column_at = lax.broadcasted_iota(jnp.int32, (1, 2 * VECS), 1)
    scales = jnp.zeros((VECS, 1), jnp.float32)
    for j in range(VECS):
        pivot_row = work[j : j + 1, :]
        pivot = work[j : j + 1, j : j + 1]
        if floor:
            pivot = jnp.maximum(pivot, jnp.maximum(floor * gram[j : j + 1, j : j + 1], 1e-30))
            pivot_row = jnp.where(column_at == j, pivot, pivot_row)
            work = jnp.where(row_at == j, pivot_row, work)
        ratio = jnp.where(row_at > j, work[:, j : j + 1] / pivot, 0.0)
        scales = jnp.where(row_at == j, lax.rsqrt(pivot), scales)
        work = work - ratio * pivot_row
    work = work * scales
    upper = jnp.where(rows <= columns, work[:, :VECS], 0.0)
    return upper, work[:, VECS:]


def first_kernel(order_ref, pieces_ref, state_ref, scaled_ref, gram_ref, upper_ref):
    drive = pieces_ref[0] + pieces_ref[1] + pieces_ref[2] + pieces_ref[3]
    state = jnp.tanh(SCALE * drive[VECS : VECS + 1])
    grown = (SCALE * (1.0 - state * state)) * drive[:VECS]
    inputs = pieces_ref[order_ref[0]][GRAM_ROW:, :128]
    for k in range(1, Y):
        inputs += pieces_ref[order_ref[k]][GRAM_ROW:, :128]
    upper, inverse = factor(unpack_gram(inputs), 1e-6)
    scaled = dot(inverse, grown)
    state_ref[...] = state
    scaled_ref[...] = scaled
    gram_ref[...] = pack_gram(gram_of(scaled))
    upper_ref[...] = upper


def second_kernel(grams_ref, scaled_ref, input_upper_ref, result_ref, product_ref, upper_ref):
    gram = unpack_gram(jnp.sum(grams_ref[...], axis=0))
    near_upper, inverse = factor(gram)
    first = dot(inverse, scaled_ref[...])
    upper = dot(near_upper, input_upper_ref[...])
    gram_two = lax.dot_general(
        dot(inverse, gram),
        inverse,
        (((1,), (1,)), ((), ())),
        precision=HIGH,
        preferred_element_type=jnp.float32,
    )
    second_upper, second_inverse = factor(gram_two)
    result_ref[...] = dot(second_inverse, first)
    product_ref[...] = dot(second_upper, upper)
    upper_ref[...] = upper


def spread_to(value, axes, count):
    return lax.all_to_all(jnp.broadcast_to(value, (count, *value.shape)), axes, 0, 0)


def gather_grams(gram):
    near = jnp.sum(spread_to(gram, ("x", "core"), X * CORE), axis=0)
    return spread_to(near, ("z", "y"), Z * Y)


def per_device(tangent, activity, block_keys):
    group = lax.axis_index("x") * CORE + lax.axis_index("core")
    z, y = lax.axis_index("z"), lax.axis_index("y")
    keys = block_keys[0]
    digits = [jnp.bitwise_and(shift_right(keys, 8 * k), 255).astype(jnp.bfloat16) for k in range(4)]
    digits = jnp.concatenate(digits + [jnp.zeros(OWN - 4 * KEYS, jnp.bfloat16)])
    own = jnp.concatenate(
        (
            tangent,
            activity.reshape(1, -1),
            digits.reshape(1, -1),
            jnp.zeros((PAD - VECS - 2, OWN), jnp.bfloat16),
        ),
        axis=0,
    )
    near = lax.all_gather(own, ("x", "core"), axis=1, tiled=True)
    vectors = lax.all_gather(near, "z")
    row_ids = group * (N // (X * CORE)) + z * ROWS + jnp.arange(ROWS, dtype=jnp.int32)
    row_terms = (row_ids * 374761393).reshape(1, ROWS)
    here = base_values(keys[None], z[None], y)
    partial = partial_drive(jnp.zeros(1, jnp.int32), row_terms, here, near[None])
    digits = lax.dynamic_slice(vectors, (0, VECS + 1, group * OWN), (Z, 1, 4 * KEYS))
    digits = digits.reshape(Z, 4, KEYS).astype(jnp.int32)
    keys = digits[:, 0] + digits[:, 1] * 256 + digits[:, 2] * 65536 + digits[:, 3] * 16777216
    bases = base_values(keys, jnp.arange(Z, dtype=jnp.int32), y)
    others = (z + jnp.arange(1, Z, dtype=jnp.int32)) % Z
    partial = partial_drive(others, row_terms, bases, vectors, (partial,))

    pieces = []
    for shift in range(Y):
        to = (y + shift) % Y
        piece = lax.dynamic_slice_in_dim(partial, to * OWN, OWN, 1)
        if shift:
            piece = lax.ppermute(piece, "y", [(i, (i + shift) % Y) for i in range(Y)])
        pieces.append(piece)

    order = (y - jnp.arange(Y, dtype=jnp.int32)) % Y
    vmem = pl.BlockSpec(memory_space=pltpu.VMEM)
    square = jax.ShapeDtypeStruct((VECS, VECS), jnp.float32)
    wide = jax.ShapeDtypeStruct((VECS, OWN), jnp.float32)
    state, scaled, gram, input_upper = pl.pallas_call(
        first_kernel,
        in_specs=[pl.BlockSpec(memory_space=pltpu.SMEM), vmem],
        out_shape=(
            jax.ShapeDtypeStruct((1, OWN), jnp.float32),
            wide,
            jax.ShapeDtypeStruct((8, 128), jnp.float32),
            square,
        ),
    )(order, jnp.stack(pieces))
    result, product, upper = pl.pallas_call(second_kernel, out_shape=(wide, square, square))(
        gather_grams(gram), scaled, input_upper
    )
    return result, state.reshape(OWN), product, upper


def solution(mesh):
    split = Mesh(mesh.devices.reshape(X, CORE, Z, Y), ("x", "core", "z", "y"))
    columns, rows = ("z", "y", "x", "core"), ("x", "core", "z", "y")
    return jax.shard_map(
        per_device,
        mesh=split,
        in_specs=(P(None, columns), P(columns), P(("x", "core"), ("z", "y"))),
        out_specs=(P(None, rows), P(rows), P(), P()),
        check_vma=False,
    )
```

```python
import functools
import math

import jax
import jax.numpy as jnp
from jax import lax
from jax.experimental import pallas as pl
from jax.experimental.pallas import tpu as pltpu
from jax.sharding import Mesh
from jax.sharding import PartitionSpec as P

N = 131072
VECS = 32
PAD = 48
KEYCOLS = 256
X, CORE, Z, Y = 4, 2, 8, 4
OWN = N // (X * CORE * Z * Y)
ROWS = OWN * Y
SEG = OWN * X * CORE
GROUP = 32
SPARE = 40
GRAM_ROW = 40
LANES = 512
KEYS = SEG // KEYCOLS
GRAM_TILE = 4 * (KEYS // 8)
SCALE = 2.0 / math.sqrt(5461.25 * N)
HIGH = lax.Precision.HIGHEST
VMEM_LIMIT = 48 * 2**20


def shift_right(value, amount):
    return lax.shift_right_logical(value, jnp.full(value.shape, amount, jnp.int32))


def coupling(value):
    value = value ^ shift_right(value, 15)
    value = value * jnp.int32(739982445)
    value = value ^ shift_right(value, 13)
    value = value * jnp.int32(695872825)
    value = value ^ shift_right(value, 16)
    return (value.astype(jnp.int8) ^ jnp.int8(-128)).astype(jnp.bfloat16)


def spare_tile(block_ref, tile):
    return block_ref[SPARE - 8 : SPARE + 8, 128 * tile : 128 * tile + 128].astype(jnp.float32)[8:]


def block_kernel(near_ref, digits_ref, block_ref):
    block_ref[...] = near_ref[...]
    own = near_ref[:VECS, :]
    gram = lax.dot_general(own, own, (((1,), (1,)), ((), ())), preferred_element_type=jnp.float32)
    rest = pack_gram(gram / N)
    tiles = [digits_ref[:, 128 * k : 128 * k + 128] for k in range(GRAM_TILE)]
    for _ in range(3):
        part = rest.astype(jnp.bfloat16).astype(jnp.float32)
        tiles.append(part)
        rest = rest - part
    for k, tile in enumerate(tiles):
        lanes = slice(128 * k, 128 * k + 128)
        above = near_ref[SPARE - 8 : SPARE + 8, lanes].astype(jnp.float32)[:8]
        block_ref[SPARE - 8 : SPARE + 8, lanes] = jnp.concatenate((above, tile)).astype(jnp.bfloat16)


def drive_kernel(places_ref, rows_ref, *refs, blocks, earlier):
    block_refs = refs[:blocks]
    earlier_refs = refs[blocks : blocks + 2 * earlier]
    out_ref, grams_ref, vectors_ref, bases_ref = refs[blocks + 2 * earlier :]
    groups = SEG // GROUP

    @pl.when(pl.program_id(0) == 0)
    def _():
        for slot in range(Z):
            if earlier:
                grams_ref[slot] = earlier_refs[1][slot]
            else:
                grams_ref[slot] = jnp.zeros((8, 128), jnp.float32)
        steps = lax.broadcasted_iota(jnp.int32, (8, 128), 0) * jnp.int32(GROUP)
        for k in range(blocks):
            place = places_ref[k]
            vectors_ref[k] = block_refs[k][...]
            gram = jnp.zeros((8, 128), jnp.float32)
            for part in range(3):
                gram = gram + spare_tile(block_refs[k], GRAM_TILE + part)
            grams_ref[place] = gram
            first_column = (place * Y + places_ref[Z]) * SEG
            for part in range(KEYS // 8):
                keys = jnp.zeros((8, 128), jnp.int32)
                for digit in range(4):
                    tile = spare_tile(block_refs[k], digit * (KEYS // 8) + part)
                    keys = keys + tile.astype(jnp.int32) * jnp.int32(256**digit)
                for row in range(8):
                    key = part * 8 + row
                    columns = first_column + key * KEYCOLS + steps
                    at = k * groups + key * 8
                    bases_ref[at : at + 8, :] = keys[row : row + 1] + columns * jnp.int32(668265261)

    spread = lax.broadcasted_iota(jnp.int32, (GROUP, 128), 0) * jnp.int32(668265261)
    starts = [rows_ref[:, 128 * k : 128 * k + 128] + spread for k in range(LANES // 128)]

    def body(number, total):
        first = pl.multiple_of(number * groups, groups)
        parts = []
        for group in range(groups):
            base = bases_ref[pl.ds(first + group, 1), :]
            parts.append(jnp.concatenate([coupling(base + start) for start in starts], axis=1))
        return total + jnp.dot(
            vectors_ref[number],
            jnp.concatenate(parts, axis=0),
            preferred_element_type=jnp.float32,
        )

    initial = earlier_refs[0][...] if earlier else jnp.zeros(out_ref.shape, jnp.float32)
    out_ref[...] = lax.fori_loop(0, blocks, body, initial)
    gram = grams_ref[0]
    for slot in range(1, Z):
        gram = gram + grams_ref[slot]
    out_ref[GRAM_ROW:, :128] = gram


def partial_drive(places, row_terms, blocks, earlier=()):
    lanes = pl.BlockSpec((PAD, LANES), lambda i: (0, i))
    grams = pl.BlockSpec((Z, 8, 128), lambda i: (0, 0, 0))
    count = len(blocks)
    return pl.pallas_call(
        functools.partial(drive_kernel, blocks=count, earlier=len(earlier) // 2),
        grid=(ROWS // LANES,),
        in_specs=[
            pl.BlockSpec(memory_space=pltpu.SMEM),
            pl.BlockSpec((1, LANES), lambda i: (0, i)),
        ]
        + [pl.BlockSpec((PAD, SEG), lambda i: (0, 0))] * count
        + [lanes, grams][: len(earlier)],
        out_specs=(lanes, grams),
        out_shape=(
            jax.ShapeDtypeStruct((PAD, ROWS), jnp.float32),
            jax.ShapeDtypeStruct((Z, 8, 128), jnp.float32),
        ),
        scratch_shapes=[
            pltpu.VMEM((count, PAD, SEG), jnp.bfloat16),
            pltpu.VMEM((count * SEG // GROUP, 128), jnp.int32),
        ],
        cost_estimate=pl.CostEstimate(
            flops=count * SEG * ROWS * 1500, bytes_accessed=count * PAD * SEG * 2, transcendentals=0
        ),
        compiler_params=pltpu.CompilerParams(vmem_limit_bytes=VMEM_LIMIT),
    )(places, row_terms, *blocks, *earlier)


def pack_gram(gram):
    return jnp.concatenate([gram[8 * k : 8 * k + 8] for k in range(4)], axis=1)


def unpack_gram(packed):
    return jnp.concatenate([packed[:, 32 * k : 32 * k + 32] for k in range(4)], axis=0)


def gram_of(rows):
    return lax.dot_general(
        rows, rows, (((1,), (1,)), ((), ())), precision=HIGH, preferred_element_type=jnp.float32
    ) / N


def dot(left, right):
    return jnp.dot(left, right, precision=HIGH, preferred_element_type=jnp.float32)


def factor(gram, floor=0.0):
    rows = lax.broadcasted_iota(jnp.int32, (VECS, VECS), 0)
    columns = lax.broadcasted_iota(jnp.int32, (VECS, VECS), 1)
    work = jnp.concatenate((gram, (rows == columns).astype(jnp.float32)), axis=1)
    row_at = lax.broadcasted_iota(jnp.int32, (VECS, 1), 0)
    column_at = lax.broadcasted_iota(jnp.int32, (1, 2 * VECS), 1)
    scales = jnp.zeros((VECS, 1), jnp.float32)
    for j in range(VECS):
        pivot_row = work[j : j + 1, :]
        pivot = work[j : j + 1, j : j + 1]
        if floor:
            pivot = jnp.maximum(pivot, jnp.maximum(floor * gram[j : j + 1, j : j + 1], 1e-30))
            pivot_row = jnp.where(column_at == j, pivot, pivot_row)
            work = jnp.where(row_at == j, pivot_row, work)
        ratio = jnp.where(row_at > j, work[:, j : j + 1] / pivot, 0.0)
        scales = jnp.where(row_at == j, lax.rsqrt(pivot), scales)
        work = work - ratio * pivot_row
    work = work * scales
    upper = jnp.where(rows <= columns, work[:, :VECS], 0.0)
    return upper, work[:, VECS:]


def first_kernel(order_ref, pieces_ref, state_ref, scaled_ref, gram_ref, upper_ref):
    drive = pieces_ref[0] + pieces_ref[1] + pieces_ref[2] + pieces_ref[3]
    state = jnp.tanh(SCALE * drive[VECS : VECS + 1])
    grown = (SCALE * (1.0 - state * state)) * drive[:VECS]
    inputs = pieces_ref[order_ref[0]][GRAM_ROW:, :128]
    for k in range(1, Y):
        inputs += pieces_ref[order_ref[k]][GRAM_ROW:, :128]
    upper, inverse = factor(unpack_gram(inputs), 1e-6)
    scaled = dot(inverse, grown)
    state_ref[...] = state
    scaled_ref[...] = scaled
    gram_ref[...] = pack_gram(gram_of(scaled))
    upper_ref[...] = upper


def second_kernel(grams_ref, scaled_ref, input_upper_ref, result_ref, product_ref, upper_ref):
    gram = unpack_gram(jnp.sum(grams_ref[...], axis=0))
    near_upper, inverse = factor(gram)
    first = dot(inverse, scaled_ref[...])
    upper = dot(near_upper, input_upper_ref[...])
    gram_two = lax.dot_general(
        dot(inverse, gram),
        inverse,
        (((1,), (1,)), ((), ())),
        precision=HIGH,
        preferred_element_type=jnp.float32,
    )
    second_upper, second_inverse = factor(gram_two)
    result_ref[...] = dot(second_inverse, first)
    product_ref[...] = dot(second_upper, upper)
    upper_ref[...] = upper


def spread_to(value, axes, count):
    return lax.all_to_all(jnp.broadcast_to(value, (count, *value.shape)), axes, 0, 0)


def gather_grams(gram):
    near = jnp.sum(spread_to(gram, ("x", "core"), X * CORE), axis=0)
    return spread_to(near, ("z", "y"), Z * Y)


def per_device(tangent, activity, block_keys):
    group = lax.axis_index("x") * CORE + lax.axis_index("core")
    z, y = lax.axis_index("z"), lax.axis_index("y")
    own = jnp.concatenate(
        (tangent, activity.reshape(1, -1), jnp.zeros((PAD - VECS - 1, OWN), jnp.bfloat16)), axis=0
    )
    near = lax.all_gather(own, ("x", "core"), axis=1, tiled=True)
    keys = block_keys[0].reshape(KEYS // 8, 8).T
    digits = [jnp.bitwise_and(shift_right(keys, 8 * k), 255) for k in range(4)]
    digits = jnp.repeat(jnp.concatenate(digits, axis=1).astype(jnp.float32), 128, axis=1)
    near = pl.pallas_call(
        block_kernel, out_shape=jax.ShapeDtypeStruct((PAD, SEG), jnp.bfloat16)
    )(near, digits)
    row_ids = group * (N // (X * CORE)) + z * ROWS + jnp.arange(ROWS, dtype=jnp.int32)
    row_terms = (row_ids * 374761393).reshape(1, ROWS)

    def places(shifts):
        shifts = jnp.array(shifts + [0] * (Z - len(shifts)), jnp.int32)
        return jnp.append((z + shifts) % Z, y)

    up = [(i, (i + 1) % Z) for i in range(Z)]
    down = [(i, (i - 1) % Z) for i in range(Z)]
    below, above = lax.ppermute(near, "z", up), lax.ppermute(near, "z", down)
    earlier = partial_drive(places([0]), row_terms, [near])
    for step in range(1, Z // 2):
        next_below = lax.ppermute(below, "z", up)
        next_above = lax.ppermute(above, "z", down) if step + 1 < Z // 2 else None
        earlier = partial_drive(places([-step, step]), row_terms, [below, above], earlier)
        below, above = next_below, next_above
    partial, _ = partial_drive(places([Z // 2]), row_terms, [below], earlier)

    pieces = []
    for shift in range(Y):
        to = (y + shift) % Y
        piece = lax.dynamic_slice_in_dim(partial, to * OWN, OWN, 1)
        if shift:
            piece = lax.ppermute(piece, "y", [(i, (i + shift) % Y) for i in range(Y)])
        pieces.append(piece)

    order = (y - jnp.arange(Y, dtype=jnp.int32)) % Y
    vmem = pl.BlockSpec(memory_space=pltpu.VMEM)
    square = jax.ShapeDtypeStruct((VECS, VECS), jnp.float32)
    wide = jax.ShapeDtypeStruct((VECS, OWN), jnp.float32)
    state, scaled, gram, input_upper = pl.pallas_call(
        first_kernel,
        in_specs=[pl.BlockSpec(memory_space=pltpu.SMEM), vmem],
        out_shape=(
            jax.ShapeDtypeStruct((1, OWN), jnp.float32),
            wide,
            jax.ShapeDtypeStruct((8, 128), jnp.float32),
            square,
        ),
    )(order, jnp.stack(pieces))
    result, product, upper = pl.pallas_call(second_kernel, out_shape=(wide, square, square))(
        gather_grams(gram), scaled, input_upper
    )
    return result, state.reshape(OWN), product, upper


def solution(mesh):
    split = Mesh(mesh.devices.reshape(X, CORE, Z, Y), ("x", "core", "z", "y"))
    columns, rows = ("z", "y", "x", "core"), ("x", "core", "z", "y")
    return jax.shard_map(
        per_device,
        mesh=split,
        in_specs=(P(None, columns), P(columns), P(("x", "core"), ("z", "y"))),
        out_specs=(P(None, rows), P(rows), P(), P()),
        check_vma=False,
    )
```

```python
import functools
import math

import jax
import jax.numpy as jnp
from jax import lax
from jax.experimental import pallas as pl
from jax.experimental.pallas import tpu as pltpu
from jax.sharding import Mesh
from jax.sharding import PartitionSpec as P

N = 131072
VECS = 32
PAD = 48
KEYCOLS = 256
X, CORE, Z, Y = 4, 2, 8, 4
OWN = N // (X * CORE * Z * Y)
ROWS = OWN * Y
SEG = OWN * X * CORE
GROUP = 32
SPARE = 40
GRAM_ROW = 40
LANES = 512
KEYS = SEG // KEYCOLS
GRAM_TILE = 4 * (KEYS // 8)
SCALE = 2.0 / math.sqrt(5461.25 * N)
HIGH = lax.Precision.HIGHEST
VMEM_LIMIT = 48 * 2**20
STEP = 16
X_AT, CORE_AT, Z_AT, Y_AT = range(4)
VMEM = pl.BlockSpec(memory_space=pltpu.VMEM)
SMEM = pl.BlockSpec(memory_space=pltpu.SMEM)


def shift_right(value, amount):
    return lax.shift_right_logical(value, jnp.full(value.shape, amount, jnp.int32))


def coupling(value):
    value = value ^ shift_right(value, 15)
    value = value * jnp.int32(739982445)
    value = value ^ shift_right(value, 13)
    value = value * jnp.int32(695872825)
    value = value ^ shift_right(value, 16)
    return (value.astype(jnp.int8) ^ jnp.int8(-128)).astype(jnp.bfloat16)


def spare_tile(block_ref, tile):
    return block_ref[SPARE - 8 : SPARE + 8, 128 * tile : 128 * tile + 128].astype(jnp.float32)[8:]


def pair_kernel(at_ref, tangent_ref, activity_ref, other_ref, pair_ref):
    rest = jnp.concatenate(
        (activity_ref[...].astype(jnp.float32), jnp.zeros((PAD - VECS - 1, OWN), jnp.float32))
    )
    here = pl.ds(pl.multiple_of(at_ref[CORE_AT] * OWN, OWN), OWN)
    there = pl.ds(pl.multiple_of((1 - at_ref[CORE_AT]) * OWN, OWN), OWN)
    pair_ref[:VECS, here] = tangent_ref[...]
    pair_ref[VECS:, here] = rest.astype(jnp.bfloat16)
    pair_ref[:, there] = other_ref[...]


def own_kernel(tangent_ref, activity_ref, own_ref):
    rest = jnp.concatenate(
        (activity_ref[...].astype(jnp.float32), jnp.zeros((PAD - VECS - 1, OWN), jnp.float32))
    )
    own_ref[:VECS, :] = tangent_ref[...]
    own_ref[VECS:, :] = rest.astype(jnp.bfloat16)


def block_kernel(at_ref, keys_ref, *refs):
    pair_refs, block_ref = refs[:X], refs[X]
    wide = CORE * OWN
    for shift in range(X):
        chip = lax.rem(at_ref[X_AT] + X - shift, X)
        block_ref[:, pl.ds(pl.multiple_of(chip * wide, wide), wide)] = pair_refs[shift][...]
    own = block_ref[:VECS, :]
    gram = lax.dot_general(own, own, (((1,), (1,)), ((), ())), preferred_element_type=jnp.float32)
    rest = pack_gram(gram / N)
    rows = lax.broadcasted_iota(jnp.int32, (8, 128), 0)
    parts = []
    for part in range(KEYS // 8):
        keys = jnp.zeros((8, 128), jnp.int32)
        for row in range(8):
            keys = jnp.where(rows == row, keys_ref[0, part * 8 + row], keys)
        parts.append(keys)
    tiles = []
    for digit in range(4):
        for keys in parts:
            tiles.append(jnp.bitwise_and(shift_right(keys, 8 * digit), 255).astype(jnp.float32))
    for _ in range(3):
        part = rest.astype(jnp.bfloat16).astype(jnp.float32)
        tiles.append(part)
        rest = rest - part
    for k, tile in enumerate(tiles):
        lanes = slice(128 * k, 128 * k + 128)
        above = block_ref[SPARE - 8 : SPARE + 8, lanes].astype(jnp.float32)[:8]
        block_ref[SPARE - 8 : SPARE + 8, lanes] = jnp.concatenate((above, tile)).astype(jnp.bfloat16)


def drive_kernel(at_ref, *refs, shifts, earlier):
    blocks = len(shifts)
    block_refs = refs[:blocks]
    earlier_refs = refs[blocks : blocks + 2 * earlier]
    out_ref, grams_ref, vectors_ref, bases_ref = refs[blocks + 2 * earlier :]
    groups = SEG // GROUP

    for slot in range(Z):
        grams_ref[slot] = earlier_refs[1][slot] if earlier else jnp.zeros((8, 128), jnp.float32)
    steps = lax.broadcasted_iota(jnp.int32, (8, 128), 0) * jnp.int32(GROUP)
    for k, shift in enumerate(shifts):
        place = lax.rem(at_ref[Z_AT] + (Z + shift), Z)
        vectors_ref[k] = block_refs[k][...]
        gram = jnp.zeros((8, 128), jnp.float32)
        for part in range(3):
            gram = gram + spare_tile(block_refs[k], GRAM_TILE + part)
        grams_ref[place] = gram
        first_column = (place * Y + at_ref[Y_AT]) * SEG
        for part in range(KEYS // 8):
            keys = jnp.zeros((8, 128), jnp.int32)
            for digit in range(4):
                tile = spare_tile(block_refs[k], digit * (KEYS // 8) + part)
                keys = keys + tile.astype(jnp.int32) * jnp.int32(256**digit)
            for row in range(8):
                key = part * 8 + row
                columns = first_column + key * KEYCOLS + steps
                at = k * groups + key * 8
                bases_ref[at : at + 8, :] = keys[row : row + 1] + columns * jnp.int32(668265261)

    first_row = (at_ref[X_AT] * CORE + at_ref[CORE_AT]) * (N // (X * CORE)) + at_ref[Z_AT] * ROWS
    row_at = lax.broadcasted_iota(jnp.int32, (GROUP, 128), 1)
    spread = lax.broadcasted_iota(jnp.int32, (GROUP, 128), 0) * jnp.int32(668265261)

    def lanes_body(part, carry):
        lane = pl.multiple_of(part * LANES, LANES)
        starts = [
            (first_row + lane + 128 * k + row_at) * jnp.int32(374761393) + spread
            for k in range(LANES // 128)
        ]

        def body(number, total):
            first = pl.multiple_of(number * groups, groups)
            parts = []
            for group in range(groups):
                base = bases_ref[pl.ds(first + group, 1), :]
                parts.append(jnp.concatenate([coupling(base + start) for start in starts], axis=1))
            return total + jnp.dot(
                vectors_ref[number],
                jnp.concatenate(parts, axis=0),
                preferred_element_type=jnp.float32,
            )

        here = pl.ds(lane, LANES)
        initial = earlier_refs[0][:, here] if earlier else jnp.zeros((PAD, LANES), jnp.float32)
        out_ref[:, here] = lax.fori_loop(0, blocks, body, initial)
        return carry

    lax.fori_loop(0, ROWS // LANES, lanes_body, 0)
    gram = grams_ref[0]
    for slot in range(1, Z):
        gram = gram + grams_ref[slot]
    for part in range(Y):
        out_ref[GRAM_ROW:, part * OWN : part * OWN + 128] = gram


def partial_drive(at, shifts, blocks, earlier=()):
    count = len(blocks)
    return pl.pallas_call(
        functools.partial(drive_kernel, shifts=shifts, earlier=len(earlier) // 2),
        in_specs=[SMEM] + [VMEM] * (count + len(earlier)),
        out_specs=(VMEM, VMEM),
        out_shape=(
            jax.ShapeDtypeStruct((PAD, ROWS), jnp.float32),
            jax.ShapeDtypeStruct((Z, 8, 128), jnp.float32),
        ),
        scratch_shapes=[
            pltpu.VMEM((count, PAD, SEG), jnp.bfloat16),
            pltpu.VMEM((count * SEG // GROUP, 128), jnp.int32),
        ],
        cost_estimate=pl.CostEstimate(
            flops=count * SEG * ROWS * 1500, bytes_accessed=count * PAD * SEG * 2, transcendentals=0
        ),
        compiler_params=pltpu.CompilerParams(vmem_limit_bytes=VMEM_LIMIT),
    )(at, *blocks, *earlier)


def pack_gram(gram):
    return jnp.concatenate([gram[8 * k : 8 * k + 8] for k in range(4)], axis=1)


def unpack_gram(packed):
    return jnp.concatenate([packed[:, 32 * k : 32 * k + 32] for k in range(4)], axis=0)


def gram_of(rows):
    return lax.dot_general(
        rows, rows, (((1,), (1,)), ((), ())), precision=HIGH, preferred_element_type=jnp.float32
    ) / N


def dot(left, right):
    return jnp.dot(left, right, precision=HIGH, preferred_element_type=jnp.float32)


def factor(gram, floor=0.0):
    rows = lax.broadcasted_iota(jnp.int32, (VECS, VECS), 0)
    columns = lax.broadcasted_iota(jnp.int32, (VECS, VECS), 1)
    wide = (VECS, 2 * VECS)
    row_at = lax.broadcasted_iota(jnp.int32, wide, 0)
    work = jnp.concatenate((gram, (rows == columns).astype(jnp.float32)), axis=1)
    scales = jnp.zeros(wide, jnp.float32)
    for first in range(0, VECS, STEP):
        spread = [
            jnp.broadcast_to(work[:, first + k : first + k + 1], wide) for k in range(STEP)
        ]
        ratios = []
        for k in range(STEP):
            at = first + k
            column = spread[k]
            for m in range(k):
                element = jnp.broadcast_to(column[first + m : first + m + 1], wide)
                column = column - ratios[m] * element
            pivot = jnp.broadcast_to(column[at : at + 1], wide)
            if floor:
                least = jnp.maximum(floor * gram[at : at + 1, at : at + 1], 1e-30)
                pivot = jnp.maximum(pivot, least)
            ratios.append(jnp.where(row_at > at, column / pivot, 0.0))
            scales = jnp.where(row_at == at, lax.rsqrt(pivot), scales)
        for k in range(STEP):
            work = work - ratios[k] * jnp.broadcast_to(work[first + k : first + k + 1], wide)
    diagonal = jnp.where(rows == columns, 1.0 / scales[:, :VECS], 0.0)
    work = work * scales
    upper = jnp.where(rows < columns, work[:, :VECS], diagonal)
    return upper, work[:, VECS:]


def first_kernel(at_ref, mine_ref, others_ref, *refs):
    others_ref, refs = (others_ref, *refs[: Y - 2]), refs[Y - 2 :]
    state_ref, scaled_ref, gram_ref, upper_ref, inputs_ref = refs
    drive = mine_ref[...]
    inputs_ref[at_ref[Y_AT]] = drive[GRAM_ROW:, :128]
    for shift, other_ref in enumerate(others_ref, 1):
        drive = drive + other_ref[...]
        inputs_ref[lax.rem(at_ref[Y_AT] + (Y - shift), Y)] = other_ref[GRAM_ROW:, :128]
    state = jnp.tanh(SCALE * drive[VECS : VECS + 1])
    grown = (SCALE * (1.0 - state * state)) * drive[:VECS]
    inputs = inputs_ref[0]
    for k in range(1, Y):
        inputs = inputs + inputs_ref[k]
    upper, inverse = factor(unpack_gram(inputs), 1e-6)
    scaled = dot(inverse, grown)
    state_ref[...] = state
    scaled_ref[...] = scaled
    gram_ref[...] = pack_gram(gram_of(scaled))
    upper_ref[...] = upper


def second_kernel(grams_ref, scaled_ref, input_upper_ref, result_ref, product_ref, upper_ref):
    gram = unpack_gram(jnp.sum(grams_ref[...], axis=0))
    near_upper, inverse = factor(gram)
    first = dot(inverse, scaled_ref[...])
    upper = dot(near_upper, input_upper_ref[...])
    gram_two = lax.dot_general(
        dot(inverse, gram),
        inverse,
        (((1,), (1,)), ((), ())),
        precision=HIGH,
        preferred_element_type=jnp.float32,
    )
    second_upper, second_inverse = factor(gram_two)
    result_ref[...] = dot(second_inverse, first)
    product_ref[...] = dot(second_upper, upper)
    upper_ref[...] = upper


def spread_to(value, axes, count):
    return lax.all_to_all(jnp.broadcast_to(value, (count, *value.shape)), axes, 0, 0)


def gather_grams(gram):
    near = jnp.sum(spread_to(gram, ("x", "core"), X * CORE), axis=0)
    return spread_to(near, ("z", "y"), Z * Y)


def per_device(tangent, activity, block_keys):
    y = lax.axis_index("y")
    at = jnp.stack([lax.axis_index(axis) for axis in ("x", "core", "z", "y")]).astype(jnp.int32)
    activity = activity.reshape(1, -1)
    block = jax.ShapeDtypeStruct((PAD, OWN), jnp.bfloat16)
    own = pl.pallas_call(own_kernel, out_shape=block)(tangent, activity)
    other = lax.ppermute(own, "core", [(0, 1), (1, 0)])
    pair = pl.pallas_call(
        pair_kernel,
        in_specs=[SMEM, VMEM, VMEM, VMEM],
        out_shape=jax.ShapeDtypeStruct((PAD, CORE * OWN), jnp.bfloat16),
    )(at, tangent, activity, other)
    pairs = [pair] + [
        lax.ppermute(pair, "x", [(i, (i + shift) % X) for i in range(X)]) for shift in range(1, X)
    ]
    near = pl.pallas_call(
        block_kernel,
        in_specs=[SMEM, SMEM] + [VMEM] * X,
        out_shape=jax.ShapeDtypeStruct((PAD, SEG), jnp.bfloat16),
    )(at, block_keys, *pairs)

    up = [(i, (i + 1) % Z) for i in range(Z)]
    down = [(i, (i - 1) % Z) for i in range(Z)]
    below, above = lax.ppermute(near, "z", up), lax.ppermute(near, "z", down)
    earlier = partial_drive(at, (0,), [near])
    for step in range(1, Z // 2):
        next_below = lax.ppermute(below, "z", up)
        next_above = lax.ppermute(above, "z", down) if step + 1 < Z // 2 else None
        earlier = partial_drive(at, (-step, step), [below, above], earlier)
        below, above = next_below, next_above
    partial, _ = partial_drive(at, (Z // 2,), [below], earlier)

    pieces = []
    for shift in range(Y):
        to = (y + shift) % Y
        piece = lax.dynamic_slice_in_dim(partial, to * OWN, OWN, 1)
        if shift:
            piece = lax.ppermute(piece, "y", [(i, (i + shift) % Y) for i in range(Y)])
        pieces.append(piece)

    square = jax.ShapeDtypeStruct((VECS, VECS), jnp.float32)
    wide = jax.ShapeDtypeStruct((VECS, OWN), jnp.float32)
    state, scaled, gram, input_upper = pl.pallas_call(
        first_kernel,
        in_specs=[SMEM] + [VMEM] * Y,
        out_shape=(
            jax.ShapeDtypeStruct((1, OWN), jnp.float32),
            wide,
            jax.ShapeDtypeStruct((8, 128), jnp.float32),
            square,
        ),
        scratch_shapes=[pltpu.VMEM((Y, 8, 128), jnp.float32)],
    )(at, *pieces)
    result, product, upper = pl.pallas_call(second_kernel, out_shape=(wide, square, square))(
        gather_grams(gram), scaled, input_upper
    )
    return result, state.reshape(OWN), product, upper


def solution(mesh):
    split = Mesh(mesh.devices.reshape(X, CORE, Z, Y), ("x", "core", "z", "y"))
    columns, rows = ("z", "y", "x", "core"), ("x", "core", "z", "y")
    return jax.shard_map(
        per_device,
        mesh=split,
        in_specs=(P(None, columns), P(columns), P(("x", "core"), ("z", "y"))),
        out_specs=(P(None, rows), P(rows), P(), P()),
        check_vma=False,
    )
```

```python
import functools
import math

import jax
import jax.numpy as jnp
from jax import lax
from jax.experimental import pallas as pl
from jax.experimental.pallas import tpu as pltpu
from jax.sharding import Mesh
from jax.sharding import PartitionSpec as P

N = 131072
VECS = 32
PAD = 48
KEYCOLS = 256
X, CORE, Z, Y = 4, 2, 8, 4
OWN = N // (X * CORE * Z * Y)
ROWS = OWN * Y
SEG = OWN * X * CORE
GROUP = 32
SPARE = 40
SENT = 40
GRAM_ROW = 36
LANES = 512
KEYS = SEG // KEYCOLS
GRAM_TILE = 4 * (KEYS // 8)
SCALE = 2.0 / math.sqrt(5461.25 * N)
HIGH = lax.Precision.HIGHEST
VMEM_LIMIT = 48 * 2**20
STEP = 16
VMEM = pl.BlockSpec(memory_space=pltpu.VMEM)
SMEM = pl.BlockSpec(memory_space=pltpu.SMEM)


def shift_right(value, amount):
    return lax.shift_right_logical(value, jnp.full(value.shape, amount, jnp.int32))


def coupling(value):
    value = value ^ shift_right(value, 15)
    value = value * jnp.int32(739982445)
    value = value ^ shift_right(value, 13)
    value = value * jnp.int32(695872825)
    value = value ^ shift_right(value, 16)
    return (value.astype(jnp.int8) ^ jnp.int8(-128)).astype(jnp.bfloat16)


def spare_tile(block_ref, tile):
    return block_ref[SPARE - 8 : SPARE + 8, 128 * tile : 128 * tile + 128].astype(jnp.float32)[8:]


def block_kernel(keys_ref, *refs):
    pair_refs, block_ref = refs[:X], refs[X]
    wide = CORE * OWN
    for shift in range(X):
        chip = lax.rem(lax.axis_index("x") + X - shift, X)
        block_ref[:, pl.ds(pl.multiple_of(chip * wide, wide), wide)] = pair_refs[shift][...]
    own = block_ref[:VECS, :]
    gram = lax.dot_general(own, own, (((1,), (1,)), ((), ())), preferred_element_type=jnp.float32)
    rest = pack_gram(gram / N)
    rows = lax.broadcasted_iota(jnp.int32, (8, 128), 0)
    parts = []
    for part in range(KEYS // 8):
        keys = jnp.zeros((8, 128), jnp.int32)
        for row in range(8):
            keys = jnp.where(rows == row, keys_ref[0, part * 8 + row], keys)
        parts.append(keys)
    tiles = []
    for digit in range(4):
        for keys in parts:
            tiles.append(jnp.bitwise_and(shift_right(keys, 8 * digit), 255).astype(jnp.float32))
    for _ in range(3):
        part = rest.astype(jnp.bfloat16).astype(jnp.float32)
        tiles.append(part)
        rest = rest - part
    for k, tile in enumerate(tiles):
        lanes = slice(128 * k, 128 * k + 128)
        above = block_ref[SPARE - 8 : SPARE + 8, lanes].astype(jnp.float32)[:8]
        block_ref[SPARE - 8 : SPARE + 8, lanes] = jnp.concatenate((above, tile)).astype(jnp.bfloat16)


def drive_kernel(*refs, shifts, earlier, last):
    blocks = len(shifts)
    block_refs = refs[:blocks]
    earlier_refs = refs[blocks : blocks + 2 * earlier]
    *out_refs, grams_ref, total_ref, vectors_ref, bases_ref = refs[blocks + 2 * earlier :]
    groups = SEG // GROUP

    for slot in range(Z):
        grams_ref[slot] = earlier_refs[1][slot] if earlier else jnp.zeros((8, 128), jnp.float32)
    steps = lax.broadcasted_iota(jnp.int32, (8, 128), 0) * jnp.int32(GROUP)
    for k, shift in enumerate(shifts):
        place = lax.rem(lax.axis_index("z") + (Z + shift), Z)
        vectors_ref[k] = block_refs[k][...]
        gram = jnp.zeros((8, 128), jnp.float32)
        for part in range(3):
            gram = gram + spare_tile(block_refs[k], GRAM_TILE + part)
        grams_ref[place] = gram
        first_column = (place * Y + lax.axis_index("y")) * SEG
        for part in range(KEYS // 8):
            keys = jnp.zeros((8, 128), jnp.int32)
            for digit in range(4):
                tile = spare_tile(block_refs[k], digit * (KEYS // 8) + part)
                keys = keys + tile.astype(jnp.int32) * jnp.int32(256**digit)
            for row in range(8):
                key = part * 8 + row
                columns = first_column + key * KEYCOLS + steps
                at = k * groups + key * 8
                bases_ref[at : at + 8, :] = keys[row : row + 1] + columns * jnp.int32(668265261)

    first_row = (lax.axis_index("x") * CORE + lax.axis_index("core")) * (N // (X * CORE)) + lax.axis_index("z") * ROWS
    row_at = lax.broadcasted_iota(jnp.int32, (GROUP, 128), 1)
    spread = lax.broadcasted_iota(jnp.int32, (GROUP, 128), 0) * jnp.int32(668265261)

    def lanes_body(part, carry):
        lane = pl.multiple_of(part * LANES, LANES)
        starts = [
            (first_row + lane + 128 * k + row_at) * jnp.int32(374761393) + spread
            for k in range(LANES // 128)
        ]

        def body(number, total):
            first = pl.multiple_of(number * groups, groups)
            parts = []
            for group in range(groups):
                base = bases_ref[pl.ds(first + group, 1), :]
                parts.append(jnp.concatenate([coupling(base + start) for start in starts], axis=1))
            return total + jnp.dot(
                vectors_ref[number],
                jnp.concatenate(parts, axis=0),
                preferred_element_type=jnp.float32,
            )

        here = pl.ds(lane, LANES)
        initial = earlier_refs[0][:, here] if earlier else jnp.zeros((PAD, LANES), jnp.float32)
        for number in range(blocks):
            initial = body(number, initial)
        total_ref[:, here] = initial
        return carry

    lax.fori_loop(0, ROWS // LANES, lanes_body, 0)
    if not last:
        out_refs[0][...] = total_ref[...]
        return
    gram = grams_ref[0]
    for slot in range(1, Z):
        gram = gram + grams_ref[slot]
    for shift, out_ref in enumerate(out_refs):
        to = lax.rem(lax.axis_index("y") + shift, Y)
        out_ref[...] = total_ref[:SENT, pl.ds(pl.multiple_of(to * OWN, OWN), OWN)]
        out_ref[GRAM_ROW:, :128] = gram[:4]
        out_ref[GRAM_ROW:, 128:256] = gram[4:]


def partial_drive(shifts, blocks, earlier=(), last=False):
    count = len(blocks)
    drive = jax.ShapeDtypeStruct((PAD, ROWS), jnp.float32)
    if last:
        out_shape = [jax.ShapeDtypeStruct((SENT, OWN), jnp.float32)] * Y
    else:
        out_shape = [drive]
    grams = jax.ShapeDtypeStruct((Z, 8, 128), jnp.float32)
    return pl.pallas_call(
        functools.partial(drive_kernel, shifts=shifts, earlier=len(earlier) // 2, last=last),
        in_specs=[VMEM] * (count + len(earlier)),
        out_specs=[VMEM] * (len(out_shape) + 1),
        out_shape=out_shape + [grams],
        scratch_shapes=[
            pltpu.VMEM(drive.shape, jnp.float32),
            pltpu.VMEM((count, PAD, SEG), jnp.bfloat16),
            pltpu.VMEM((count * SEG // GROUP, 128), jnp.int32),
        ],
        cost_estimate=pl.CostEstimate(
            flops=count * SEG * ROWS * 1500, bytes_accessed=count * PAD * SEG * 2, transcendentals=0
        ),
        compiler_params=pltpu.CompilerParams(vmem_limit_bytes=VMEM_LIMIT),
    )(*blocks, *earlier)


def pack_gram(gram):
    return jnp.concatenate([gram[8 * k : 8 * k + 8] for k in range(4)], axis=1)


def unpack_gram(packed):
    return jnp.concatenate([packed[:, 32 * k : 32 * k + 32] for k in range(4)], axis=0)


def gram_of(rows):
    return lax.dot_general(
        rows, rows, (((1,), (1,)), ((), ())), precision=HIGH, preferred_element_type=jnp.float32
    ) / N


def dot(left, right):
    return jnp.dot(left, right, precision=HIGH, preferred_element_type=jnp.float32)


def factor(gram, floor=0.0):
    rows = lax.broadcasted_iota(jnp.int32, (VECS, VECS), 0)
    columns = lax.broadcasted_iota(jnp.int32, (VECS, VECS), 1)
    wide = (VECS, 2 * VECS)
    row_at = lax.broadcasted_iota(jnp.int32, wide, 0)
    work = jnp.concatenate((gram, (rows == columns).astype(jnp.float32)), axis=1)
    scales = jnp.zeros(wide, jnp.float32)
    for first in range(0, VECS, STEP):
        spread = [
            jnp.broadcast_to(work[:, first + k : first + k + 1], wide) for k in range(STEP)
        ]
        ratios = []
        for k in range(STEP):
            at = first + k
            column = spread[k]
            for m in range(k):
                element = jnp.broadcast_to(column[first + m : first + m + 1], wide)
                column = column - ratios[m] * element
            pivot = jnp.broadcast_to(column[at : at + 1], wide)
            if floor:
                least = jnp.maximum(floor * gram[at : at + 1, at : at + 1], 1e-30)
                pivot = jnp.maximum(pivot, least)
            ratios.append(jnp.where(row_at > at, column / pivot, 0.0))
            scales = jnp.where(row_at == at, lax.rsqrt(pivot), scales)
        for k in range(STEP):
            work = work - ratios[k] * jnp.broadcast_to(work[first + k : first + k + 1], wide)
    diagonal = jnp.where(rows == columns, 1.0 / scales[:, :VECS], 0.0)
    work = work * scales
    upper = jnp.where(rows < columns, work[:, :VECS], diagonal)
    return upper, work[:, VECS:]


def first_kernel(mine_ref, others_ref, *refs):
    others_ref, refs = (others_ref, *refs[: Y - 2]), refs[Y - 2 :]
    state_ref, scaled_ref, gram_ref, upper_ref, inputs_ref = refs
    drive = mine_ref[...]

    def gram_part(piece):
        return jnp.concatenate((piece[GRAM_ROW:, :128], piece[GRAM_ROW:, 128:256]))

    inputs_ref[lax.axis_index("y")] = gram_part(drive)
    for shift, other_ref in enumerate(others_ref, 1):
        other = other_ref[...]
        drive = drive + other
        inputs_ref[lax.rem(lax.axis_index("y") + (Y - shift), Y)] = gram_part(other)
    state = jnp.tanh(SCALE * drive[VECS : VECS + 1])
    grown = (SCALE * (1.0 - state * state)) * drive[:VECS]
    inputs = inputs_ref[0]
    for k in range(1, Y):
        inputs = inputs + inputs_ref[k]
    upper, inverse = factor(unpack_gram(inputs), 1e-6)
    scaled = dot(inverse, grown)
    state_ref[...] = state
    scaled_ref[...] = scaled
    gram_ref[...] = jnp.broadcast_to(pack_gram(gram_of(scaled)), gram_ref.shape)
    upper_ref[...] = upper


def second_kernel(grams_ref, scaled_ref, input_upper_ref, result_ref, product_ref, upper_ref):
    gram = unpack_gram(jnp.sum(grams_ref[...], axis=0))
    near_upper, inverse = factor(gram)
    first = dot(inverse, scaled_ref[...])
    upper = dot(near_upper, input_upper_ref[...])
    gram_two = lax.dot_general(
        dot(inverse, gram),
        inverse,
        (((1,), (1,)), ((), ())),
        precision=HIGH,
        preferred_element_type=jnp.float32,
    )
    second_upper, second_inverse = factor(gram_two)
    result_ref[...] = dot(second_inverse, first)
    product_ref[...] = dot(second_upper, upper)
    upper_ref[...] = upper


def gather_grams(copies):
    near = jnp.sum(lax.all_to_all(copies, ("x", "core"), 0, 0), axis=0)
    copies = jnp.broadcast_to(near, (Z * Y, *near.shape))
    return lax.all_to_all(copies, ("z", "y"), 0, 0)


def per_device(tangent, activity, block_keys):
    own = jnp.concatenate(
        (tangent, activity.reshape(1, -1), jnp.zeros((PAD - VECS - 1, OWN), jnp.bfloat16)), axis=0
    )
    other = lax.ppermute(own, "core", [(0, 1), (1, 0)])
    pair = jnp.where(
        lax.axis_index("core") == 0,
        jnp.concatenate((own, other), axis=1),
        jnp.concatenate((other, own), axis=1),
    )
    pairs = [pair] + [
        lax.ppermute(pair, "x", [(i, (i + shift) % X) for i in range(X)]) for shift in range(1, X)
    ]
    near = pl.pallas_call(
        block_kernel,
        in_specs=[SMEM] + [VMEM] * X,
        out_shape=jax.ShapeDtypeStruct((PAD, SEG), jnp.bfloat16),
    )(block_keys, *pairs)

    up = [(i, (i + 1) % Z) for i in range(Z)]
    down = [(i, (i - 1) % Z) for i in range(Z)]
    below, above = lax.ppermute(near, "z", up), lax.ppermute(near, "z", down)
    earlier = partial_drive((0,), [near])
    for step in range(1, Z // 2):
        next_below = lax.ppermute(below, "z", up)
        next_above = lax.ppermute(above, "z", down) if step + 1 < Z // 2 else None
        earlier = partial_drive((-step, step), [below, above], earlier)
        below, above = next_below, next_above
    *pieces, _ = partial_drive((Z // 2,), [below], earlier, last=True)
    for shift in range(1, Y):
        pieces[shift] = lax.ppermute(pieces[shift], "y", [(i, (i + shift) % Y) for i in range(Y)])

    square = jax.ShapeDtypeStruct((VECS, VECS), jnp.float32)
    wide = jax.ShapeDtypeStruct((VECS, OWN), jnp.float32)
    state, scaled, gram, input_upper = pl.pallas_call(
        first_kernel,
        out_shape=(
            jax.ShapeDtypeStruct((1, OWN), jnp.float32),
            wide,
            jax.ShapeDtypeStruct((X * CORE, 8, 128), jnp.float32),
            square,
        ),
        scratch_shapes=[pltpu.VMEM((Y, 8, 128), jnp.float32)],
    )(*pieces)
    result, product, upper = pl.pallas_call(second_kernel, out_shape=(wide, square, square))(
        gather_grams(gram), scaled, input_upper
    )
    return result, state.reshape(OWN), product, upper


def solution(mesh):
    split = Mesh(mesh.devices.reshape(X, CORE, Z, Y), ("x", "core", "z", "y"))
    columns, rows = ("z", "y", "x", "core"), ("x", "core", "z", "y")
    return jax.shard_map(
        per_device,
        mesh=split,
        in_specs=(P(None, columns), P(columns), P(("x", "core"), ("z", "y"))),
        out_specs=(P(None, rows), P(rows), P(), P()),
        check_vma=False,
    )
```

```python
import functools
import math

import jax
import jax.numpy as jnp
from jax import lax
from jax.experimental import pallas as pl
from jax.experimental.pallas import tpu as pltpu
from jax.sharding import Mesh
from jax.sharding import PartitionSpec as P

N = 131072
VECS = 32
PAD = 48
KEYCOLS = 256
X, CORE, Z, Y = 4, 2, 8, 4
OWN = N // (X * CORE * Z * Y)
ROWS = OWN * Y
SEG = OWN * X * CORE
GROUP = 32
SPARE = 40
SENT = 40
GRAM_ROW = 36
LANES = 512
KEYS = SEG // KEYCOLS
GRAM_TILE = 4 * (KEYS // 8)
SCALE = 2.0 / math.sqrt(5461.25 * N)
HIGH = lax.Precision.HIGHEST
PARAMS = pltpu.CompilerParams(vmem_limit_bytes=16 * 2**20)
STEP = 16
VMEM = pl.BlockSpec(memory_space=pltpu.VMEM)
SMEM = pl.BlockSpec(memory_space=pltpu.SMEM)


def shift_right(value, amount):
    return lax.shift_right_logical(value, jnp.full(value.shape, amount, jnp.int32))


def coupling(value):
    value = value ^ shift_right(value, 15)
    value = value * jnp.int32(739982445)
    value = value ^ shift_right(value, 13)
    value = value * jnp.int32(695872825)
    value = value ^ shift_right(value, 16)
    return (value.astype(jnp.int8) ^ jnp.int8(-128)).astype(jnp.bfloat16)


def spare_tile(block_ref, tile):
    return block_ref[SPARE - 8 : SPARE + 8, 128 * tile : 128 * tile + 128].astype(jnp.float32)[8:]


def block_kernel(keys_ref, *refs):
    pair_refs, block_ref = refs[:X], refs[X]
    wide = CORE * OWN
    for shift in range(X):
        chip = lax.rem(lax.axis_index("x") + X - shift, X)
        block_ref[:, pl.ds(pl.multiple_of(chip * wide, wide), wide)] = pair_refs[shift][...]
    own = block_ref[:VECS, :]
    gram = lax.dot_general(own, own, (((1,), (1,)), ((), ())), preferred_element_type=jnp.float32)
    rest = pack_gram(gram / N)
    rows = lax.broadcasted_iota(jnp.int32, (8, 128), 0)
    parts = []
    for part in range(KEYS // 8):
        keys = jnp.zeros((8, 128), jnp.int32)
        for row in range(8):
            keys = jnp.where(rows == row, keys_ref[0, part * 8 + row], keys)
        parts.append(keys)
    tiles = []
    for digit in range(4):
        for keys in parts:
            tiles.append(jnp.bitwise_and(shift_right(keys, 8 * digit), 255).astype(jnp.float32))
    for _ in range(3):
        part = rest.astype(jnp.bfloat16).astype(jnp.float32)
        tiles.append(part)
        rest = rest - part
    for k, tile in enumerate(tiles):
        lanes = slice(128 * k, 128 * k + 128)
        above = block_ref[SPARE - 8 : SPARE + 8, lanes].astype(jnp.float32)[:8]
        block_ref[SPARE - 8 : SPARE + 8, lanes] = jnp.concatenate((above, tile)).astype(jnp.bfloat16)


def drive_kernel(*refs, shifts, earlier, last):
    blocks = len(shifts)
    block_refs = refs[:blocks]
    earlier_refs = refs[blocks : blocks + 2 * earlier]
    *out_refs, grams_ref, total_ref, vectors_ref, bases_ref = refs[blocks + 2 * earlier :]
    groups = SEG // GROUP

    for slot in range(Z):
        grams_ref[slot] = earlier_refs[1][slot] if earlier else jnp.zeros((8, 128), jnp.float32)
    steps = lax.broadcasted_iota(jnp.int32, (8, 128), 0) * jnp.int32(GROUP)
    for k, shift in enumerate(shifts):
        place = lax.rem(lax.axis_index("z") + (Z + shift), Z)
        vectors_ref[k] = block_refs[k][...]
        gram = jnp.zeros((8, 128), jnp.float32)
        for part in range(3):
            gram = gram + spare_tile(block_refs[k], GRAM_TILE + part)
        grams_ref[place] = gram
        first_column = (place * Y + lax.axis_index("y")) * SEG
        for part in range(KEYS // 8):
            keys = jnp.zeros((8, 128), jnp.int32)
            for digit in range(4):
                tile = spare_tile(block_refs[k], digit * (KEYS // 8) + part)
                keys = keys + tile.astype(jnp.int32) * jnp.int32(256**digit)
            for row in range(8):
                key = part * 8 + row
                columns = first_column + key * KEYCOLS + steps
                at = k * groups + key * 8
                bases_ref[at : at + 8, :] = keys[row : row + 1] + columns * jnp.int32(668265261)

    first_row = (lax.axis_index("x") * CORE + lax.axis_index("core")) * (N // (X * CORE)) + lax.axis_index("z") * ROWS
    row_at = lax.broadcasted_iota(jnp.int32, (GROUP, 128), 1)
    spread = lax.broadcasted_iota(jnp.int32, (GROUP, 128), 0) * jnp.int32(668265261)

    def lanes_body(part, carry):
        lane = pl.multiple_of(part * LANES, LANES)
        starts = [
            (first_row + lane + 128 * k + row_at) * jnp.int32(374761393) + spread
            for k in range(LANES // 128)
        ]

        def body(number, total):
            first = pl.multiple_of(number * groups, groups)
            parts = []
            for group in range(groups):
                base = bases_ref[pl.ds(first + group, 1), :]
                parts.append(jnp.concatenate([coupling(base + start) for start in starts], axis=1))
            return total + jnp.dot(
                vectors_ref[number],
                jnp.concatenate(parts, axis=0),
                preferred_element_type=jnp.float32,
            )

        here = pl.ds(lane, LANES)
        initial = earlier_refs[0][:, here] if earlier else jnp.zeros((PAD, LANES), jnp.float32)
        total_ref[:, here] = lax.fori_loop(0, blocks, body, initial)
        return carry

    lax.fori_loop(0, ROWS // LANES, lanes_body, 0)
    if not last:
        out_refs[0][...] = total_ref[...]
        return
    gram = grams_ref[0]
    for slot in range(1, Z):
        gram = gram + grams_ref[slot]
    for shift, out_ref in enumerate(out_refs):
        to = lax.rem(lax.axis_index("y") + shift, Y)
        out_ref[...] = total_ref[:SENT, pl.ds(pl.multiple_of(to * OWN, OWN), OWN)]
        out_ref[GRAM_ROW:, :128] = gram[:4]
        out_ref[GRAM_ROW:, 128:256] = gram[4:]


def partial_drive(shifts, blocks, earlier=(), last=False):
    count = len(blocks)
    drive = jax.ShapeDtypeStruct((PAD, ROWS), jnp.float32)
    if last:
        out_shape = [jax.ShapeDtypeStruct((SENT, OWN), jnp.float32)] * Y
    else:
        out_shape = [drive]
    grams = jax.ShapeDtypeStruct((Z, 8, 128), jnp.float32)
    return pl.pallas_call(
        functools.partial(drive_kernel, shifts=shifts, earlier=len(earlier) // 2, last=last),
        in_specs=[VMEM] * (count + len(earlier)),
        out_specs=[VMEM] * (len(out_shape) + 1),
        out_shape=out_shape + [grams],
        scratch_shapes=[
            pltpu.VMEM(drive.shape, jnp.float32),
            pltpu.VMEM((count, PAD, SEG), jnp.bfloat16),
            pltpu.VMEM((count * SEG // GROUP, 128), jnp.int32),
        ],
        cost_estimate=pl.CostEstimate(
            flops=count * SEG * ROWS * 1500, bytes_accessed=count * PAD * SEG * 2, transcendentals=0
        ),
        compiler_params=PARAMS,
    )(*blocks, *earlier)


def pack_gram(gram):
    return jnp.concatenate([gram[8 * k : 8 * k + 8] for k in range(4)], axis=1)


def unpack_gram(packed):
    return jnp.concatenate([packed[:, 32 * k : 32 * k + 32] for k in range(4)], axis=0)


def gram_of(rows):
    return lax.dot_general(
        rows, rows, (((1,), (1,)), ((), ())), precision=HIGH, preferred_element_type=jnp.float32
    ) / N


def dot(left, right):
    return jnp.dot(left, right, precision=HIGH, preferred_element_type=jnp.float32)


def factor(gram, floor=0.0):
    rows = lax.broadcasted_iota(jnp.int32, (VECS, VECS), 0)
    columns = lax.broadcasted_iota(jnp.int32, (VECS, VECS), 1)
    wide = (VECS, 2 * VECS)
    row_at = lax.broadcasted_iota(jnp.int32, wide, 0)
    work = jnp.concatenate((gram, (rows == columns).astype(jnp.float32)), axis=1)
    scales = jnp.zeros(wide, jnp.float32)
    for first in range(0, VECS, STEP):
        spread = [
            jnp.broadcast_to(work[:, first + k : first + k + 1], wide) for k in range(STEP)
        ]
        ratios = []
        for k in range(STEP):
            at = first + k
            column = spread[k]
            for m in range(k):
                element = jnp.broadcast_to(column[first + m : first + m + 1], wide)
                column = column - ratios[m] * element
            pivot = jnp.broadcast_to(column[at : at + 1], wide)
            if floor:
                least = jnp.maximum(floor * gram[at : at + 1, at : at + 1], 1e-30)
                pivot = jnp.maximum(pivot, least)
            ratios.append(jnp.where(row_at > at, column / pivot, 0.0))
            scales = jnp.where(row_at == at, lax.rsqrt(pivot), scales)
        for k in range(STEP):
            work = work - ratios[k] * jnp.broadcast_to(work[first + k : first + k + 1], wide)
    diagonal = jnp.where(rows == columns, 1.0 / scales[:, :VECS], 0.0)
    work = work * scales
    upper = jnp.where(rows < columns, work[:, :VECS], diagonal)
    return upper, work[:, VECS:]


def first_kernel(mine_ref, others_ref, *refs):
    others_ref, refs = (others_ref, *refs[: Y - 2]), refs[Y - 2 :]
    state_ref, scaled_ref, gram_ref, upper_ref, inputs_ref = refs
    drive = mine_ref[...]

    def gram_part(piece):
        return jnp.concatenate((piece[GRAM_ROW:, :128], piece[GRAM_ROW:, 128:256]))

    inputs_ref[lax.axis_index("y")] = gram_part(drive)
    for shift, other_ref in enumerate(others_ref, 1):
        other = other_ref[...]
        drive = drive + other
        inputs_ref[lax.rem(lax.axis_index("y") + (Y - shift), Y)] = gram_part(other)
    state = jnp.tanh(SCALE * drive[VECS : VECS + 1])
    grown = (SCALE * (1.0 - state * state)) * drive[:VECS]
    inputs = inputs_ref[0]
    for k in range(1, Y):
        inputs = inputs + inputs_ref[k]
    upper, inverse = factor(unpack_gram(inputs), 1e-6)
    scaled = dot(inverse, grown)
    state_ref[...] = state
    scaled_ref[...] = scaled
    gram_ref[...] = jnp.broadcast_to(pack_gram(gram_of(scaled)), gram_ref.shape)
    upper_ref[...] = upper


def second_kernel(grams_ref, scaled_ref, input_upper_ref, result_ref, product_ref, upper_ref):
    gram = unpack_gram(jnp.sum(grams_ref[...], axis=0))
    near_upper, inverse = factor(gram)
    first = dot(inverse, scaled_ref[...])
    upper = dot(near_upper, input_upper_ref[...])
    gram_two = lax.dot_general(
        dot(inverse, gram),
        inverse,
        (((1,), (1,)), ((), ())),
        precision=HIGH,
        preferred_element_type=jnp.float32,
    )
    second_upper, second_inverse = factor(gram_two)
    result_ref[...] = dot(second_inverse, first)
    product_ref[...] = dot(second_upper, upper)
    upper_ref[...] = upper


def gather_grams(copies):
    near = jnp.sum(lax.all_to_all(copies, ("x", "core", "y"), 0, 0), axis=0)
    return lax.all_to_all(jnp.broadcast_to(near, (Z, *near.shape)), "z", 0, 0)


def per_device(tangent, activity, block_keys):
    own = jnp.concatenate(
        (tangent, activity.reshape(1, -1), jnp.zeros((PAD - VECS - 1, OWN), jnp.bfloat16)), axis=0
    )
    other = lax.ppermute(own, "core", [(0, 1), (1, 0)])
    pair = jnp.where(
        lax.axis_index("core") == 0,
        jnp.concatenate((own, other), axis=1),
        jnp.concatenate((other, own), axis=1),
    )
    pairs = [pair] + [
        lax.ppermute(pair, "x", [(i, (i + shift) % X) for i in range(X)]) for shift in range(1, X)
    ]
    near = pl.pallas_call(
        block_kernel,
        in_specs=[SMEM] + [VMEM] * X,
        out_shape=jax.ShapeDtypeStruct((PAD, SEG), jnp.bfloat16),
        compiler_params=PARAMS,
    )(block_keys, *pairs)

    up = [(i, (i + 1) % Z) for i in range(Z)]
    down = [(i, (i - 1) % Z) for i in range(Z)]
    below, above = lax.ppermute(near, "z", up), lax.ppermute(near, "z", down)
    earlier = partial_drive((0,), [near])
    for step in range(1, Z // 2):
        next_below = lax.ppermute(below, "z", up)
        next_above = lax.ppermute(above, "z", down) if step + 1 < Z // 2 else None
        earlier = partial_drive((-step, step), [below, above], earlier)
        below, above = next_below, next_above
    *pieces, _ = partial_drive((Z // 2,), [below], earlier, last=True)
    for shift in range(1, Y):
        pieces[shift] = lax.ppermute(pieces[shift], "y", [(i, (i + shift) % Y) for i in range(Y)])

    square = jax.ShapeDtypeStruct((VECS, VECS), jnp.float32)
    wide = jax.ShapeDtypeStruct((VECS, OWN), jnp.float32)
    state, scaled, gram, input_upper = pl.pallas_call(
        first_kernel,
        out_shape=(
            jax.ShapeDtypeStruct((1, OWN), jnp.float32),
            wide,
            jax.ShapeDtypeStruct((X * CORE * Y, 8, 128), jnp.float32),
            square,
        ),
        compiler_params=PARAMS,
        scratch_shapes=[pltpu.VMEM((Y, 8, 128), jnp.float32)],
    )(*pieces)
    result, product, upper = pl.pallas_call(
        second_kernel, out_shape=(wide, square, square), compiler_params=PARAMS
    )(gather_grams(gram), scaled, input_upper)
    return result, state.reshape(OWN), product, upper


def solution(mesh):
    split = Mesh(mesh.devices.reshape(X, CORE, Z, Y), ("x", "core", "z", "y"))
    columns, rows = ("z", "y", "x", "core"), ("x", "core", "z", "y")
    return jax.shard_map(
        per_device,
        mesh=split,
        in_specs=(P(None, columns), P(columns), P(("x", "core"), ("z", "y"))),
        out_specs=(P(None, rows), P(rows), P(), P()),
        check_vma=False,
    )
```

```python
import functools
import math

import jax
import jax.numpy as jnp
from jax import lax
from jax.experimental import pallas as pl
from jax.experimental.pallas import tpu as pltpu
from jax.sharding import Mesh
from jax.sharding import PartitionSpec as P

N = 131072
VECS = 32
PAD = 48
KEYCOLS = 256
X, CORE, Z, Y = 4, 2, 8, 4
OWN = N // (X * CORE * Z * Y)
ROWS = OWN * Y
SEG = OWN * X * CORE
GROUP = 32
SPARE = 40
SENT = 40
GRAM_ROW = 36
LANES = 512
KEYS = SEG // KEYCOLS
GRAM_TILE = 4 * (KEYS // 8)
SCALE = 2.0 / math.sqrt(5461.25 * N)
HIGH = lax.Precision.HIGHEST
PARAMS = pltpu.CompilerParams(vmem_limit_bytes=16 * 2**20)
STEP = 16
VMEM = pl.BlockSpec(memory_space=pltpu.VMEM)
SMEM = pl.BlockSpec(memory_space=pltpu.SMEM)


def shift_right(value, amount):
    return lax.shift_right_logical(value, jnp.full(value.shape, amount, jnp.int32))


def coupling(value):
    value = value ^ shift_right(value, 15)
    value = value * jnp.int32(739982445)
    value = value ^ shift_right(value, 13)
    value = value * jnp.int32(695872825)
    value = value ^ shift_right(value, 16)
    return (value.astype(jnp.int8) ^ jnp.int8(-128)).astype(jnp.bfloat16)


def spare_tile(block_ref, tile):
    return block_ref[SPARE - 8 : SPARE + 8, 128 * tile : 128 * tile + 128].astype(jnp.float32)[8:]


def own_kernel(tangent_ref, activity_ref, own_ref):
    parts = [activity_ref[k : k + 1, :].astype(jnp.float32) for k in range(OWN // 128)]
    rest = jnp.zeros((PAD - VECS - 1, OWN), jnp.float32)
    rest = jnp.concatenate((jnp.concatenate(parts, axis=1), rest))
    own_ref[:VECS, :] = tangent_ref[...]
    own_ref[VECS:, :] = rest.astype(jnp.bfloat16)


def block_kernel(keys_ref, mine_ref, others_ref, block_ref):
    shards_refs = (mine_ref, others_ref)
    for core in range(CORE):
        at = jnp.bitwise_xor(lax.axis_index("core"), core) * OWN
        for shift in range(X):
            chip = lax.rem(lax.axis_index("x") + (X - shift), X)
            lanes = pl.ds(pl.multiple_of(chip * (CORE * OWN) + at, OWN), OWN)
            block_ref[:, lanes] = shards_refs[core][shift]
    own = block_ref[:VECS, :]
    gram = lax.dot_general(own, own, (((1,), (1,)), ((), ())), preferred_element_type=jnp.float32)
    rest = pack_gram(gram / N)
    rows = lax.broadcasted_iota(jnp.int32, (8, 128), 0)
    parts = []
    for part in range(KEYS // 8):
        keys = jnp.zeros((8, 128), jnp.int32)
        for row in range(8):
            keys = jnp.where(rows == row, keys_ref[0, part * 8 + row], keys)
        parts.append(keys)
    tiles = []
    for digit in range(4):
        for keys in parts:
            tiles.append(jnp.bitwise_and(shift_right(keys, 8 * digit), 255).astype(jnp.float32))
    for _ in range(3):
        part = rest.astype(jnp.bfloat16).astype(jnp.float32)
        tiles.append(part)
        rest = rest - part
    for k, tile in enumerate(tiles):
        lanes = slice(128 * k, 128 * k + 128)
        above = block_ref[SPARE - 8 : SPARE + 8, lanes].astype(jnp.float32)[:8]
        block_ref[SPARE - 8 : SPARE + 8, lanes] = jnp.concatenate((above, tile)).astype(jnp.bfloat16)


def drive_kernel(*refs, shifts, earlier, parts):
    blocks = len(shifts)
    block_refs = refs[:blocks]
    earlier_refs = refs[blocks : blocks + 2 * earlier]
    *out_refs, grams_ref, total_ref, vectors_ref, bases_ref = refs[blocks + 2 * earlier :]
    groups = SEG // GROUP

    for slot in range(Z):
        grams_ref[slot] = earlier_refs[1][slot] if earlier else jnp.zeros((8, 128), jnp.float32)
    steps = lax.broadcasted_iota(jnp.int32, (8, 128), 0) * jnp.int32(GROUP)
    for k, shift in enumerate(shifts):
        place = lax.rem(lax.axis_index("z") + (Z + shift), Z)
        vectors_ref[k] = block_refs[k][...]
        gram = jnp.zeros((8, 128), jnp.float32)
        for part in range(3):
            gram = gram + spare_tile(block_refs[k], GRAM_TILE + part)
        grams_ref[place] = gram
        first_column = (place * Y + lax.axis_index("y")) * SEG
        for part in range(KEYS // 8):
            keys = jnp.zeros((8, 128), jnp.int32)
            for digit in range(4):
                tile = spare_tile(block_refs[k], digit * (KEYS // 8) + part)
                keys = keys + tile.astype(jnp.int32) * jnp.int32(256**digit)
            for row in range(8):
                key = part * 8 + row
                columns = first_column + key * KEYCOLS + steps
                at = k * groups + key * 8
                bases_ref[at : at + 8, :] = keys[row : row + 1] + columns * jnp.int32(668265261)

    def part_at(number):
        return lax.rem(lax.axis_index("y") + (parts[0] + number), Y) if parts else number

    first_row = (lax.axis_index("x") * CORE + lax.axis_index("core")) * (N // (X * CORE)) + lax.axis_index("z") * ROWS
    row_at = lax.broadcasted_iota(jnp.int32, (GROUP, 128), 1)
    spread = lax.broadcasted_iota(jnp.int32, (GROUP, 128), 0) * jnp.int32(668265261)

    def lanes_body(number, carry):
        lane = pl.multiple_of(part_at(number) * LANES, LANES)
        starts = [
            (first_row + lane + 128 * k + row_at) * jnp.int32(374761393) + spread
            for k in range(LANES // 128)
        ]

        def body(number, total):
            first = pl.multiple_of(number * groups, groups)
            parts = []
            for group in range(groups):
                base = bases_ref[pl.ds(first + group, 1), :]
                parts.append(jnp.concatenate([coupling(base + start) for start in starts], axis=1))
            return total + jnp.dot(
                vectors_ref[number],
                jnp.concatenate(parts, axis=0),
                preferred_element_type=jnp.float32,
            )

        here = pl.ds(lane, LANES)
        initial = earlier_refs[0][:, here] if earlier else jnp.zeros((PAD, LANES), jnp.float32)
        total_ref[:, here] = lax.fori_loop(0, blocks, body, initial)
        return carry

    lax.fori_loop(0, len(parts) or Y, lanes_body, 0)
    if not parts:
        out_refs[0][...] = total_ref[...]
        return
    gram = grams_ref[0]
    for slot in range(1, Z):
        gram = gram + grams_ref[slot]
    for number, out_ref in enumerate(out_refs):
        lane = pl.multiple_of(part_at(number) * LANES, LANES)
        out_ref[...] = total_ref[:SENT, pl.ds(lane, LANES)]
        out_ref[GRAM_ROW:, :128] = gram[:4]
        out_ref[GRAM_ROW:, 128:256] = gram[4:]


def partial_drive(shifts, blocks, earlier=(), parts=()):
    count = len(blocks)
    drive = jax.ShapeDtypeStruct((PAD, ROWS), jnp.float32)
    if parts:
        out_shape = [jax.ShapeDtypeStruct((SENT, OWN), jnp.float32)] * len(parts)
    else:
        out_shape = [drive]
    grams = jax.ShapeDtypeStruct((Z, 8, 128), jnp.float32)
    return pl.pallas_call(
        functools.partial(drive_kernel, shifts=shifts, earlier=len(earlier) // 2, parts=parts),
        in_specs=[VMEM] * (count + len(earlier)),
        out_specs=[VMEM] * (len(out_shape) + 1),
        out_shape=out_shape + [grams],
        scratch_shapes=[
            pltpu.VMEM(drive.shape, jnp.float32),
            pltpu.VMEM((count, PAD, SEG), jnp.bfloat16),
            pltpu.VMEM((count * SEG // GROUP, 128), jnp.int32),
        ],
        cost_estimate=pl.CostEstimate(
            flops=count * SEG * (len(parts) or Y) * LANES * 1500,
            bytes_accessed=count * PAD * SEG * 2,
            transcendentals=0,
        ),
        compiler_params=PARAMS,
    )(*blocks, *earlier)


def pack_gram(gram):
    return jnp.concatenate([gram[8 * k : 8 * k + 8] for k in range(4)], axis=1)


def unpack_gram(packed):
    return jnp.concatenate([packed[:, 32 * k : 32 * k + 32] for k in range(4)], axis=0)


def gram_of(rows):
    return lax.dot_general(
        rows, rows, (((1,), (1,)), ((), ())), precision=HIGH, preferred_element_type=jnp.float32
    ) / N


def dot(left, right):
    return jnp.dot(left, right, precision=HIGH, preferred_element_type=jnp.float32)


def factor(gram, floor=0.0):
    rows = lax.broadcasted_iota(jnp.int32, (VECS, VECS), 0)
    columns = lax.broadcasted_iota(jnp.int32, (VECS, VECS), 1)
    wide = (VECS, 2 * VECS)
    row_at = lax.broadcasted_iota(jnp.int32, wide, 0)
    work = jnp.concatenate((gram, (rows == columns).astype(jnp.float32)), axis=1)
    scales = jnp.zeros(wide, jnp.float32)
    for first in range(0, VECS, STEP):
        spread = [
            jnp.broadcast_to(work[:, first + k : first + k + 1], wide) for k in range(STEP)
        ]
        ratios = []
        for k in range(STEP):
            at = first + k
            column = spread[k]
            for m in range(k):
                element = jnp.broadcast_to(column[first + m : first + m + 1], wide)
                column = column - ratios[m] * element
            pivot = jnp.broadcast_to(column[at : at + 1], wide)
            if floor:
                least = jnp.maximum(floor * gram[at : at + 1, at : at + 1], 1e-30)
                pivot = jnp.maximum(pivot, least)
            ratios.append(jnp.where(row_at > at, column / pivot, 0.0))
            scales = jnp.where(row_at == at, lax.rsqrt(pivot), scales)
        for k in range(STEP):
            work = work - ratios[k] * jnp.broadcast_to(work[first + k : first + k + 1], wide)
    diagonal = jnp.where(rows == columns, 1.0 / scales[:, :VECS], 0.0)
    work = work * scales
    upper = jnp.where(rows < columns, work[:, :VECS], diagonal)
    return upper, work[:, VECS:]


def first_kernel(mine_ref, others_ref, *refs):
    others_ref, refs = (others_ref, *refs[: Y - 2]), refs[Y - 2 :]
    state_ref, scaled_ref, gram_ref, upper_ref, inputs_ref = refs
    drive = mine_ref[...]

    def gram_part(piece):
        return jnp.concatenate((piece[GRAM_ROW:, :128], piece[GRAM_ROW:, 128:256]))

    inputs_ref[lax.axis_index("y")] = gram_part(drive)
    for shift, other_ref in enumerate(others_ref, 1):
        other = other_ref[...]
        drive = drive + other
        inputs_ref[lax.rem(lax.axis_index("y") + (Y - shift), Y)] = gram_part(other)
    state = jnp.tanh(SCALE * drive[VECS : VECS + 1])
    grown = (SCALE * (1.0 - state * state)) * drive[:VECS]
    inputs = inputs_ref[0]
    for k in range(1, Y):
        inputs = inputs + inputs_ref[k]
    upper, inverse = factor(unpack_gram(inputs), 1e-6)
    scaled = dot(inverse, grown)
    state_ref[...] = state
    scaled_ref[...] = scaled
    gram_ref[...] = jnp.broadcast_to(pack_gram(gram_of(scaled)), gram_ref.shape)
    upper_ref[...] = upper


def second_kernel(grams_ref, scaled_ref, input_upper_ref, result_ref, product_ref, upper_ref):
    gram = unpack_gram(jnp.sum(grams_ref[...], axis=0))
    near_upper, inverse = factor(gram)
    first = dot(inverse, scaled_ref[...])
    upper = dot(near_upper, input_upper_ref[...])
    gram_two = lax.dot_general(
        dot(inverse, gram),
        inverse,
        (((1,), (1,)), ((), ())),
        precision=HIGH,
        preferred_element_type=jnp.float32,
    )
    second_upper, second_inverse = factor(gram_two)
    result_ref[...] = dot(second_inverse, first)
    product_ref[...] = dot(second_upper, upper)
    upper_ref[...] = upper


def gather_grams(copies):
    near = jnp.sum(lax.all_to_all(copies, ("x", "core", "y"), 0, 0), axis=0)
    return lax.all_to_all(jnp.broadcast_to(near, (Z, *near.shape)), "z", 0, 0)


def per_device(tangent, activity, block_keys):
    block = jax.ShapeDtypeStruct((PAD, OWN), jnp.bfloat16)
    own = pl.pallas_call(own_kernel, out_shape=block, compiler_params=PARAMS)(
        tangent, activity.reshape(OWN // 128, 128)
    )
    mine = jnp.stack(
        [own]
        + [
            lax.ppermute(own, "x", [(i, (i + shift) % X) for i in range(X)])
            for shift in range(1, X)
        ]
    )
    others = lax.ppermute(mine, "core", [(0, 1), (1, 0)])
    near = pl.pallas_call(
        block_kernel,
        in_specs=[SMEM, VMEM, VMEM],
        out_shape=jax.ShapeDtypeStruct((PAD, SEG), jnp.bfloat16),
        compiler_params=PARAMS,
    )(block_keys, mine, others)

    up = [(i, (i + 1) % Z) for i in range(Z)]
    down = [(i, (i - 1) % Z) for i in range(Z)]
    below, above = lax.ppermute(near, "z", up), lax.ppermute(near, "z", down)
    earlier = partial_drive((0,), [near])
    for step in range(1, Z // 2):
        next_below = lax.ppermute(below, "z", up)
        next_above = lax.ppermute(above, "z", down) if step + 1 < Z // 2 else None
        earlier = partial_drive((-step, step), [below, above], earlier)
        below, above = next_below, next_above
    *sent, _ = partial_drive((Z // 2,), [below], earlier, tuple(range(1, Y)))
    kept, _ = partial_drive((Z // 2,), [below], earlier, (0,))
    pieces = [kept] + [
        lax.ppermute(piece, "y", [(i, (i + shift) % Y) for i in range(Y)])
        for shift, piece in enumerate(sent, 1)
    ]

    square = jax.ShapeDtypeStruct((VECS, VECS), jnp.float32)
    wide = jax.ShapeDtypeStruct((VECS, OWN), jnp.float32)
    state, scaled, gram, input_upper = pl.pallas_call(
        first_kernel,
        out_shape=(
            jax.ShapeDtypeStruct((1, OWN), jnp.float32),
            wide,
            jax.ShapeDtypeStruct((X * CORE * Y, 8, 128), jnp.float32),
            square,
        ),
        compiler_params=PARAMS,
        scratch_shapes=[pltpu.VMEM((Y, 8, 128), jnp.float32)],
    )(*pieces)
    result, product, upper = pl.pallas_call(
        second_kernel, out_shape=(wide, square, square), compiler_params=PARAMS
    )(gather_grams(gram), scaled, input_upper)
    return result, state.reshape(OWN), product, upper


def solution(mesh):
    split = Mesh(mesh.devices.reshape(X, CORE, Z, Y), ("x", "core", "z", "y"))
    columns, rows = ("z", "y", "x", "core"), ("x", "core", "z", "y")
    return jax.shard_map(
        per_device,
        mesh=split,
        in_specs=(P(None, columns), P(columns), P(("x", "core"), ("z", "y"))),
        out_specs=(P(None, rows), P(rows), P(), P()),
        check_vma=False,
    )
```

```python
import functools
import math

import jax
import jax.numpy as jnp
from jax import lax
from jax.experimental import pallas as pl
from jax.experimental.pallas import tpu as pltpu
from jax.sharding import Mesh
from jax.sharding import PartitionSpec as P

N = 131072
VECS = 32
PAD = 48
KEYCOLS = 256
X, CORE, Z, Y = 4, 2, 8, 4
OWN = N // (X * CORE * Z * Y)
ROWS = OWN * Y
SEG = OWN * X * CORE
GROUP = 32
SPARE = 40
SENT = 40
GRAM_ROW = 36
LANES = 512
KEYS = SEG // KEYCOLS
GRAM_TILE = 4 * (KEYS // 8)
SCALE = 2.0 / math.sqrt(5461.25 * N)
HIGH = lax.Precision.HIGHEST
PARAMS = pltpu.CompilerParams(vmem_limit_bytes=16 * 2**20)
STEP = 16
VMEM = pl.BlockSpec(memory_space=pltpu.VMEM)
SMEM = pl.BlockSpec(memory_space=pltpu.SMEM)


def shift_right(value, amount):
    return lax.shift_right_logical(value, jnp.full(value.shape, amount, jnp.int32))


def coupling(value):
    value = value ^ shift_right(value, 15)
    value = value * jnp.int32(739982445)
    value = value ^ shift_right(value, 13)
    value = value * jnp.int32(695872825)
    value = value ^ shift_right(value, 16)
    return (value.astype(jnp.int8) ^ jnp.int8(-128)).astype(jnp.bfloat16)


def spare_tile(block_ref, tile):
    return block_ref[SPARE - 8 : SPARE + 8, 128 * tile : 128 * tile + 128].astype(jnp.float32)[8:]


def own_kernel(tangent_ref, activity_ref, own_ref):
    parts = [activity_ref[k : k + 1, :].astype(jnp.float32) for k in range(OWN // 128)]
    rest = jnp.zeros((PAD - VECS - 1, OWN), jnp.float32)
    rest = jnp.concatenate((jnp.concatenate(parts, axis=1), rest))
    own_ref[:VECS, :] = tangent_ref[...]
    own_ref[VECS:, :] = rest.astype(jnp.bfloat16)


def block_kernel(keys_ref, mine_ref, others_ref, block_ref):
    shards_refs = (mine_ref, others_ref)
    for core in range(CORE):
        at = jnp.bitwise_xor(lax.axis_index("core"), core) * OWN
        for shift in range(X):
            chip = lax.rem(lax.axis_index("x") + (X - shift), X)
            lanes = pl.ds(pl.multiple_of(chip * (CORE * OWN) + at, OWN), OWN)
            block_ref[:, lanes] = shards_refs[core][shift]
    own = block_ref[:VECS, :]
    gram = lax.dot_general(own, own, (((1,), (1,)), ((), ())), preferred_element_type=jnp.float32)
    rest = pack_gram(gram / N)
    rows = lax.broadcasted_iota(jnp.int32, (8, 128), 0)
    parts = []
    for part in range(KEYS // 8):
        keys = jnp.zeros((8, 128), jnp.int32)
        for row in range(8):
            keys = jnp.where(rows == row, keys_ref[0, part * 8 + row], keys)
        parts.append(keys)
    tiles = []
    for digit in range(4):
        for keys in parts:
            tiles.append(jnp.bitwise_and(shift_right(keys, 8 * digit), 255).astype(jnp.float32))
    for _ in range(3):
        part = rest.astype(jnp.bfloat16).astype(jnp.float32)
        tiles.append(part)
        rest = rest - part
    for k, tile in enumerate(tiles):
        lanes = slice(128 * k, 128 * k + 128)
        above = block_ref[SPARE - 8 : SPARE + 8, lanes].astype(jnp.float32)[:8]
        block_ref[SPARE - 8 : SPARE + 8, lanes] = jnp.concatenate((above, tile)).astype(jnp.bfloat16)


def shard_index():
    return lax.axis_index("x") * CORE + lax.axis_index("core")


def row_starts(lane):
    first_row = shard_index() * (N // (X * CORE)) + lax.axis_index("z") * ROWS + lane
    row_at = lax.broadcasted_iota(jnp.int32, (GROUP, 128), 1)
    spread = lax.broadcasted_iota(jnp.int32, (GROUP, 128), 0) * jnp.int32(668265261)
    return [
        (first_row + 128 * k + row_at) * jnp.int32(374761393) + spread
        for k in range(LANES // 128)
    ]


def product(vectors, bases, starts):
    parts = [
        jnp.concatenate([coupling(base + start) for start in starts], axis=1) for base in bases
    ]
    return jnp.dot(
        vectors, jnp.concatenate(parts, axis=0), preferred_element_type=jnp.float32
    )


def shard_kernel(keys_ref, own_ref, out_ref, bases_ref):
    shard = shard_index()
    place = lax.axis_index("z") * Y + lax.axis_index("y")
    steps = lax.broadcasted_iota(jnp.int32, (8, 128), 0) * jnp.int32(GROUP)
    for k in range(OWN // KEYCOLS):
        key = keys_ref[0, shard * (OWN // KEYCOLS) + k]
        columns = place * SEG + shard * OWN + k * KEYCOLS + steps
        bases_ref[8 * k : 8 * k + 8, :] = key + columns * jnp.int32(668265261)

    def lanes_body(number, carry):
        lane = pl.multiple_of(number * LANES, LANES)
        bases = [bases_ref[k : k + 1, :] for k in range(OWN // GROUP)]
        out_ref[:, pl.ds(lane, LANES)] = product(own_ref[...], bases, row_starts(lane))
        return carry

    lax.fori_loop(0, Y, lanes_body, 0)


def drive_kernel(*refs, shifts, earlier, parts):
    blocks = len(shifts)
    block_refs = refs[:blocks]
    earlier_refs = refs[blocks : blocks + earlier]
    *out_refs, grams_ref, total_ref, vectors_ref, bases_ref = refs[blocks + earlier :]
    groups = SEG // GROUP

    for slot in range(Z):
        grams_ref[slot] = earlier_refs[1][slot] if earlier == 2 else jnp.zeros((8, 128), jnp.float32)
    steps = lax.broadcasted_iota(jnp.int32, (8, 128), 0) * jnp.int32(GROUP)
    for k, shift in enumerate(shifts):
        place = lax.rem(lax.axis_index("z") + (Z + shift), Z)
        vectors_ref[k] = block_refs[k][...]
        gram = jnp.zeros((8, 128), jnp.float32)
        for part in range(3):
            gram = gram + spare_tile(block_refs[k], GRAM_TILE + part)
        grams_ref[place] = gram
        first_column = (place * Y + lax.axis_index("y")) * SEG
        for part in range(KEYS // 8):
            keys = jnp.zeros((8, 128), jnp.int32)
            for digit in range(4):
                tile = spare_tile(block_refs[k], digit * (KEYS // 8) + part)
                keys = keys + tile.astype(jnp.int32) * jnp.int32(256**digit)
            for row in range(8):
                key = part * 8 + row
                columns = first_column + key * KEYCOLS + steps
                at = k * groups + key * 8
                bases_ref[at : at + 8, :] = keys[row : row + 1] + columns * jnp.int32(668265261)

    def part_at(number):
        return lax.rem(lax.axis_index("y") + (parts[0] + number), Y) if parts else number

    def lanes_body(number, carry):
        lane = pl.multiple_of(part_at(number) * LANES, LANES)
        starts = row_starts(lane)

        def body(number, total):
            first = pl.multiple_of(number * groups, groups)
            bases = [bases_ref[pl.ds(first + group, 1), :] for group in range(groups)]
            return total + product(vectors_ref[number], bases, starts)

        def others_body(total):
            shards = [
                jnp.bitwise_and(shard_index() + shift, X * CORE - 1) for shift in range(1, X * CORE)
            ]
            bases = []
            vectors = []
            for shard in shards:
                first = pl.multiple_of(shard * (OWN // GROUP), OWN // GROUP)
                bases += [bases_ref[pl.ds(first + k, 1), :] for k in range(OWN // GROUP)]
                vectors.append(vectors_ref[0, :, pl.ds(pl.multiple_of(shard * OWN, OWN), OWN)])
            return total + product(jnp.concatenate(vectors, axis=1), bases, starts)

        here = pl.ds(lane, LANES)
        initial = earlier_refs[0][:, here] if earlier else jnp.zeros((PAD, LANES), jnp.float32)
        if earlier == 1:
            total_ref[:, here] = others_body(initial)
        else:
            total_ref[:, here] = lax.fori_loop(0, blocks, body, initial)
        return carry

    lax.fori_loop(0, len(parts) or Y, lanes_body, 0)
    if not parts:
        out_refs[0][...] = total_ref[...]
        return
    gram = grams_ref[0]
    for slot in range(1, Z):
        gram = gram + grams_ref[slot]
    for number, out_ref in enumerate(out_refs):
        lane = pl.multiple_of(part_at(number) * LANES, LANES)
        out_ref[...] = total_ref[:SENT, pl.ds(lane, LANES)]
        out_ref[GRAM_ROW:, :128] = gram[:4]
        out_ref[GRAM_ROW:, 128:256] = gram[4:]


def partial_drive(shifts, blocks, earlier=(), parts=()):
    count = len(blocks)
    drive = jax.ShapeDtypeStruct((PAD, ROWS), jnp.float32)
    if parts:
        out_shape = [jax.ShapeDtypeStruct((SENT, OWN), jnp.float32)] * len(parts)
    else:
        out_shape = [drive]
    grams = jax.ShapeDtypeStruct((Z, 8, 128), jnp.float32)
    return pl.pallas_call(
        functools.partial(drive_kernel, shifts=shifts, earlier=len(earlier), parts=parts),
        in_specs=[VMEM] * (count + len(earlier)),
        out_specs=[VMEM] * (len(out_shape) + 1),
        out_shape=out_shape + [grams],
        scratch_shapes=[
            pltpu.VMEM(drive.shape, jnp.float32),
            pltpu.VMEM((count, PAD, SEG), jnp.bfloat16),
            pltpu.VMEM((count * SEG // GROUP, 128), jnp.int32),
        ],
        cost_estimate=pl.CostEstimate(
            flops=count * SEG * (len(parts) or Y) * LANES * 1500,
            bytes_accessed=count * PAD * SEG * 2,
            transcendentals=0,
        ),
        compiler_params=PARAMS,
    )(*blocks, *earlier)


def pack_gram(gram):
    return jnp.concatenate([gram[8 * k : 8 * k + 8] for k in range(4)], axis=1)


def unpack_gram(packed):
    return jnp.concatenate([packed[:, 32 * k : 32 * k + 32] for k in range(4)], axis=0)


def gram_of(rows):
    return lax.dot_general(
        rows, rows, (((1,), (1,)), ((), ())), precision=HIGH, preferred_element_type=jnp.float32
    ) / N


def dot(left, right):
    return jnp.dot(left, right, precision=HIGH, preferred_element_type=jnp.float32)


def factor(gram, floor=0.0):
    rows = lax.broadcasted_iota(jnp.int32, (VECS, VECS), 0)
    columns = lax.broadcasted_iota(jnp.int32, (VECS, VECS), 1)
    wide = (VECS, 2 * VECS)
    row_at = lax.broadcasted_iota(jnp.int32, wide, 0)
    work = jnp.concatenate((gram, (rows == columns).astype(jnp.float32)), axis=1)
    scales = jnp.zeros(wide, jnp.float32)
    for first in range(0, VECS, STEP):
        spread = [
            jnp.broadcast_to(work[:, first + k : first + k + 1], wide) for k in range(STEP)
        ]
        ratios = []
        for k in range(STEP):
            at = first + k
            column = spread[k]
            for m in range(k):
                element = jnp.broadcast_to(column[first + m : first + m + 1], wide)
                column = column - ratios[m] * element
            pivot = jnp.broadcast_to(column[at : at + 1], wide)
            if floor:
                least = jnp.maximum(floor * gram[at : at + 1, at : at + 1], 1e-30)
                pivot = jnp.maximum(pivot, least)
            ratios.append(jnp.where(row_at > at, column / pivot, 0.0))
            scales = jnp.where(row_at == at, lax.rsqrt(pivot), scales)
        for k in range(STEP):
            work = work - ratios[k] * jnp.broadcast_to(work[first + k : first + k + 1], wide)
    diagonal = jnp.where(rows == columns, 1.0 / scales[:, :VECS], 0.0)
    work = work * scales
    upper = jnp.where(rows < columns, work[:, :VECS], diagonal)
    return upper, work[:, VECS:]


def first_kernel(mine_ref, others_ref, *refs):
    others_ref, refs = (others_ref, *refs[: Y - 2]), refs[Y - 2 :]
    state_ref, scaled_ref, gram_ref, upper_ref, inputs_ref = refs
    drive = mine_ref[...]

    def gram_part(piece):
        return jnp.concatenate((piece[GRAM_ROW:, :128], piece[GRAM_ROW:, 128:256]))

    inputs_ref[lax.axis_index("y")] = gram_part(drive)
    for shift, other_ref in enumerate(others_ref, 1):
        other = other_ref[...]
        drive = drive + other
        inputs_ref[lax.rem(lax.axis_index("y") + (Y - shift), Y)] = gram_part(other)
    state = jnp.tanh(SCALE * drive[VECS : VECS + 1])
    grown = (SCALE * (1.0 - state * state)) * drive[:VECS]
    inputs = inputs_ref[0]
    for k in range(1, Y):
        inputs = inputs + inputs_ref[k]
    upper, inverse = factor(unpack_gram(inputs), 1e-6)
    scaled = dot(inverse, grown)
    state_ref[...] = state
    scaled_ref[...] = scaled
    gram_ref[...] = jnp.broadcast_to(pack_gram(gram_of(scaled)), gram_ref.shape)
    upper_ref[...] = upper


def second_kernel(grams_ref, scaled_ref, input_upper_ref, result_ref, product_ref, upper_ref):
    gram = unpack_gram(jnp.sum(grams_ref[...], axis=0))
    near_upper, inverse = factor(gram)
    first = dot(inverse, scaled_ref[...])
    upper = dot(near_upper, input_upper_ref[...])
    gram_two = lax.dot_general(
        dot(inverse, gram),
        inverse,
        (((1,), (1,)), ((), ())),
        precision=HIGH,
        preferred_element_type=jnp.float32,
    )
    second_upper, second_inverse = factor(gram_two)
    result_ref[...] = dot(second_inverse, first)
    product_ref[...] = dot(second_upper, upper)
    upper_ref[...] = upper


def gather_grams(copies):
    near = jnp.sum(lax.all_to_all(copies, ("x", "core", "y"), 0, 0), axis=0)
    return lax.all_to_all(jnp.broadcast_to(near, (Z, *near.shape)), "z", 0, 0)


def per_device(tangent, activity, block_keys):
    block = jax.ShapeDtypeStruct((PAD, OWN), jnp.bfloat16)
    own = pl.pallas_call(own_kernel, out_shape=block, compiler_params=PARAMS)(
        tangent, activity.reshape(OWN // 128, 128)
    )
    shards = [
        lax.ppermute(own, "x", [(i, (i + shift) % X) for i in range(X)]) for shift in range(1, X)
    ]
    start = pl.pallas_call(
        shard_kernel,
        in_specs=[SMEM, VMEM],
        out_shape=jax.ShapeDtypeStruct((PAD, ROWS), jnp.float32),
        scratch_shapes=[pltpu.VMEM((OWN // GROUP, 128), jnp.int32)],
        cost_estimate=pl.CostEstimate(
            flops=OWN * ROWS * 1500, bytes_accessed=PAD * OWN * 2, transcendentals=0
        ),
        compiler_params=PARAMS,
    )(block_keys, own)
    shards, start = lax.optimization_barrier((shards, start))
    mine = jnp.stack([own] + shards)
    others = lax.ppermute(mine, "core", [(0, 1), (1, 0)])
    near = pl.pallas_call(
        block_kernel,
        in_specs=[SMEM, VMEM, VMEM],
        out_shape=jax.ShapeDtypeStruct((PAD, SEG), jnp.bfloat16),
        compiler_params=PARAMS,
    )(block_keys, mine, others)

    up = [(i, (i + 1) % Z) for i in range(Z)]
    down = [(i, (i - 1) % Z) for i in range(Z)]
    below, above = lax.ppermute(near, "z", up), lax.ppermute(near, "z", down)
    earlier = partial_drive((0,), [near], (start,))
    for step in range(1, Z // 2):
        next_below = lax.ppermute(below, "z", up)
        next_above = lax.ppermute(above, "z", down) if step + 1 < Z // 2 else None
        earlier = partial_drive((-step, step), [below, above], earlier)
        below, above = next_below, next_above
    *sent, _ = partial_drive((Z // 2,), [below], earlier, tuple(range(1, Y)))
    kept, _ = partial_drive((Z // 2,), [below], earlier, (0,))
    pieces = [kept] + [
        lax.ppermute(piece, "y", [(i, (i + shift) % Y) for i in range(Y)])
        for shift, piece in enumerate(sent, 1)
    ]

    square = jax.ShapeDtypeStruct((VECS, VECS), jnp.float32)
    wide = jax.ShapeDtypeStruct((VECS, OWN), jnp.float32)
    state, scaled, gram, input_upper = pl.pallas_call(
        first_kernel,
        out_shape=(
            jax.ShapeDtypeStruct((1, OWN), jnp.float32),
            wide,
            jax.ShapeDtypeStruct((X * CORE * Y, 8, 128), jnp.float32),
            square,
        ),
        compiler_params=PARAMS,
        scratch_shapes=[pltpu.VMEM((Y, 8, 128), jnp.float32)],
    )(*pieces)
    result, product, upper = pl.pallas_call(
        second_kernel, out_shape=(wide, square, square), compiler_params=PARAMS
    )(gather_grams(gram), scaled, input_upper)
    return result, state.reshape(OWN), product, upper


def solution(mesh):
    split = Mesh(mesh.devices.reshape(X, CORE, Z, Y), ("x", "core", "z", "y"))
    columns, rows = ("z", "y", "x", "core"), ("x", "core", "z", "y")
    return jax.shard_map(
        per_device,
        mesh=split,
        in_specs=(P(None, columns), P(columns), P(("x", "core"), ("z", "y"))),
        out_specs=(P(None, rows), P(rows), P(), P()),
        check_vma=False,
    )
```

```python
import functools
import math

import jax
import jax.numpy as jnp
from jax import lax
from jax.experimental import pallas as pl
from jax.experimental.pallas import tpu as pltpu
from jax.sharding import Mesh
from jax.sharding import PartitionSpec as P

N = 131072
VECS = 32
PAD = 48
KEYCOLS = 256
X, CORE, Z, Y = 4, 2, 8, 4
OWN = N // (X * CORE * Z * Y)
ROWS = OWN * Y
SEG = OWN * X * CORE
GROUP = 32
SPARE = 40
SENT = 40
GRAM_ROW = 36
LANES = 512
KEYS = SEG // KEYCOLS
GRAM_TILE = 4 * (KEYS // 8)
SCALE = 2.0 / math.sqrt(5461.25 * N)
HIGH = lax.Precision.HIGHEST
PARAMS = pltpu.CompilerParams(vmem_limit_bytes=16 * 2**20)
STEP = 16
VMEM = pl.BlockSpec(memory_space=pltpu.VMEM)
SMEM = pl.BlockSpec(memory_space=pltpu.SMEM)


def shift_right(value, amount):
    return lax.shift_right_logical(value, jnp.full(value.shape, amount, jnp.int32))


def coupling(value):
    value = value ^ shift_right(value, 15)
    value = value * jnp.int32(739982445)
    value = value ^ shift_right(value, 13)
    value = value * jnp.int32(695872825)
    value = value ^ shift_right(value, 16)
    return (value.astype(jnp.int8) ^ jnp.int8(-128)).astype(jnp.bfloat16)


def spare_tile(block_ref, tile):
    return block_ref[SPARE - 8 : SPARE + 8, 128 * tile : 128 * tile + 128].astype(jnp.float32)[8:]


def own_kernel(tangent_ref, activity_ref, own_ref):
    parts = [activity_ref[k : k + 1, :].astype(jnp.float32) for k in range(OWN // 128)]
    rest = jnp.zeros((PAD - VECS - 1, OWN), jnp.float32)
    rest = jnp.concatenate((jnp.concatenate(parts, axis=1), rest))
    own_ref[:VECS, :] = tangent_ref[...]
    own_ref[VECS:, :] = rest.astype(jnp.bfloat16)


def block_kernel(keys_ref, mine_ref, others_ref, block_ref):
    shards_refs = (mine_ref, others_ref)
    for core in range(CORE):
        at = jnp.bitwise_xor(lax.axis_index("core"), core) * OWN
        for shift in range(X):
            chip = lax.rem(lax.axis_index("x") + (X - shift), X)
            lanes = pl.ds(pl.multiple_of(chip * (CORE * OWN) + at, OWN), OWN)
            block_ref[:, lanes] = shards_refs[core][shift]
    own = block_ref[:VECS, :]
    gram = lax.dot_general(own, own, (((1,), (1,)), ((), ())), preferred_element_type=jnp.float32)
    rest = pack_gram(gram / N)
    rows = lax.broadcasted_iota(jnp.int32, (8, 128), 0)
    parts = []
    for part in range(KEYS // 8):
        keys = jnp.zeros((8, 128), jnp.int32)
        for row in range(8):
            keys = jnp.where(rows == row, keys_ref[0, part * 8 + row], keys)
        parts.append(keys)
    tiles = []
    for digit in range(4):
        for keys in parts:
            tiles.append(jnp.bitwise_and(shift_right(keys, 8 * digit), 255).astype(jnp.float32))
    for _ in range(3):
        part = rest.astype(jnp.bfloat16).astype(jnp.float32)
        tiles.append(part)
        rest = rest - part
    for k, tile in enumerate(tiles):
        lanes = slice(128 * k, 128 * k + 128)
        above = block_ref[SPARE - 8 : SPARE + 8, lanes].astype(jnp.float32)[:8]
        block_ref[SPARE - 8 : SPARE + 8, lanes] = jnp.concatenate((above, tile)).astype(jnp.bfloat16)


def shard_index():
    return lax.axis_index("x") * CORE + lax.axis_index("core")


def row_starts(lane):
    first_row = shard_index() * (N // (X * CORE)) + lax.axis_index("z") * ROWS + lane
    row_at = lax.broadcasted_iota(jnp.int32, (GROUP, 128), 1)
    spread = lax.broadcasted_iota(jnp.int32, (GROUP, 128), 0) * jnp.int32(668265261)
    return [
        (first_row + 128 * k + row_at) * jnp.int32(374761393) + spread
        for k in range(LANES // 128)
    ]


def product(vectors, bases, starts):
    parts = [
        jnp.concatenate([coupling(base + start) for start in starts], axis=1) for base in bases
    ]
    return jnp.dot(
        vectors, jnp.concatenate(parts, axis=0), preferred_element_type=jnp.float32
    )


def shard_kernel(keys_ref, own_ref, out_ref, bases_ref):
    shard = shard_index()
    place = lax.axis_index("z") * Y + lax.axis_index("y")
    steps = lax.broadcasted_iota(jnp.int32, (8, 128), 0) * jnp.int32(GROUP)
    for k in range(OWN // KEYCOLS):
        key = keys_ref[0, shard * (OWN // KEYCOLS) + k]
        columns = place * SEG + shard * OWN + k * KEYCOLS + steps
        bases_ref[8 * k : 8 * k + 8, :] = key + columns * jnp.int32(668265261)

    def lanes_body(number, carry):
        lane = pl.multiple_of(number * LANES, LANES)
        bases = [bases_ref[k : k + 1, :] for k in range(OWN // GROUP)]
        out_ref[:, pl.ds(lane, LANES)] = product(own_ref[...], bases, row_starts(lane))
        return carry

    lax.fori_loop(0, Y, lanes_body, 0)


def drive_kernel(*refs, shifts, earlier, parts, unroll):
    blocks = len(shifts)
    block_refs = refs[:blocks]
    earlier_refs = refs[blocks : blocks + earlier]
    *out_refs, grams_ref, total_ref, vectors_ref, bases_ref = refs[blocks + earlier :]
    groups = SEG // GROUP

    for slot in range(Z):
        grams_ref[slot] = earlier_refs[1][slot] if earlier == 2 else jnp.zeros((8, 128), jnp.float32)
    steps = lax.broadcasted_iota(jnp.int32, (8, 128), 0) * jnp.int32(GROUP)
    for k, shift in enumerate(shifts):
        place = lax.rem(lax.axis_index("z") + (Z + shift), Z)
        vectors_ref[k] = block_refs[k][...]
        gram = jnp.zeros((8, 128), jnp.float32)
        for part in range(3):
            gram = gram + spare_tile(block_refs[k], GRAM_TILE + part)
        grams_ref[place] = gram
        first_column = (place * Y + lax.axis_index("y")) * SEG
        for part in range(KEYS // 8):
            keys = jnp.zeros((8, 128), jnp.int32)
            for digit in range(4):
                tile = spare_tile(block_refs[k], digit * (KEYS // 8) + part)
                keys = keys + tile.astype(jnp.int32) * jnp.int32(256**digit)
            for row in range(8):
                key = part * 8 + row
                columns = first_column + key * KEYCOLS + steps
                at = k * groups + key * 8
                bases_ref[at : at + 8, :] = keys[row : row + 1] + columns * jnp.int32(668265261)

    def part_at(number):
        return lax.rem(lax.axis_index("y") + (parts[0] + number), Y) if parts else number

    def step_body(step, carry):
        number, block = lax.shift_right_logical(step, blocks - 1), jnp.bitwise_and(step, blocks - 1)
        lane = pl.multiple_of(part_at(number) * LANES, LANES)
        here = pl.ds(lane, LANES)
        if earlier == 1:
            shards = [
                jnp.bitwise_and(shard_index() + shift, X * CORE - 1) for shift in range(1, X * CORE)
            ]
            bases = []
            vectors = []
            for shard in shards:
                first = pl.multiple_of(shard * (OWN // GROUP), OWN // GROUP)
                bases += [bases_ref[pl.ds(first + k, 1), :] for k in range(OWN // GROUP)]
                vectors.append(vectors_ref[0, :, pl.ds(pl.multiple_of(shard * OWN, OWN), OWN)])
            vectors = jnp.concatenate(vectors, axis=1)
        else:
            first = pl.multiple_of(block * groups, groups)
            bases = [bases_ref[pl.ds(first + group, 1), :] for group in range(groups)]
            vectors = vectors_ref[block]
        total_ref[:, here] += product(vectors, bases, row_starts(lane))
        return carry

    total_ref[...] = earlier_refs[0][...]
    lax.fori_loop(0, (len(parts) or Y) * blocks, step_body, 0, unroll=unroll)
    if not parts:
        out_refs[0][...] = total_ref[...]
        return
    gram = grams_ref[0]
    for slot in range(1, Z):
        gram = gram + grams_ref[slot]
    for number, out_ref in enumerate(out_refs):
        lane = pl.multiple_of(part_at(number) * LANES, LANES)
        out_ref[...] = total_ref[:SENT, pl.ds(lane, LANES)]
        out_ref[GRAM_ROW:, :128] = gram[:4]
        out_ref[GRAM_ROW:, 128:256] = gram[4:]


def partial_drive(shifts, blocks, earlier=(), parts=(), unroll=1):
    count = len(blocks)
    drive = jax.ShapeDtypeStruct((PAD, ROWS), jnp.float32)
    if parts:
        out_shape = [jax.ShapeDtypeStruct((SENT, OWN), jnp.float32)] * len(parts)
    else:
        out_shape = [drive]
    grams = jax.ShapeDtypeStruct((Z, 8, 128), jnp.float32)
    return pl.pallas_call(
        functools.partial(
            drive_kernel, shifts=shifts, earlier=len(earlier), parts=parts, unroll=unroll
        ),
        in_specs=[VMEM] * (count + len(earlier)),
        out_specs=[VMEM] * (len(out_shape) + 1),
        out_shape=out_shape + [grams],
        scratch_shapes=[
            pltpu.VMEM(drive.shape, jnp.float32),
            pltpu.VMEM((count, PAD, SEG), jnp.bfloat16),
            pltpu.VMEM((count * SEG // GROUP, 128), jnp.int32),
        ],
        cost_estimate=pl.CostEstimate(
            flops=count * SEG * (len(parts) or Y) * LANES * 1500,
            bytes_accessed=count * PAD * SEG * 2,
            transcendentals=0,
        ),
        compiler_params=PARAMS,
    )(*blocks, *earlier)


def pack_gram(gram):
    return jnp.concatenate([gram[8 * k : 8 * k + 8] for k in range(4)], axis=1)


def unpack_gram(packed):
    return jnp.concatenate([packed[:, 32 * k : 32 * k + 32] for k in range(4)], axis=0)


def gram_of(rows):
    return lax.dot_general(
        rows, rows, (((1,), (1,)), ((), ())), precision=HIGH, preferred_element_type=jnp.float32
    ) / N


def dot(left, right):
    return jnp.dot(left, right, precision=HIGH, preferred_element_type=jnp.float32)


def factor(gram, floor=0.0):
    rows = lax.broadcasted_iota(jnp.int32, (VECS, VECS), 0)
    columns = lax.broadcasted_iota(jnp.int32, (VECS, VECS), 1)
    wide = (VECS, 2 * VECS)
    row_at = lax.broadcasted_iota(jnp.int32, wide, 0)
    work = jnp.concatenate((gram, (rows == columns).astype(jnp.float32)), axis=1)
    scales = jnp.zeros(wide, jnp.float32)
    for first in range(0, VECS, STEP):
        spread = [
            jnp.broadcast_to(work[:, first + k : first + k + 1], wide) for k in range(STEP)
        ]
        ratios = []
        for k in range(STEP):
            at = first + k
            column = spread[k]
            for m in range(k):
                element = jnp.broadcast_to(column[first + m : first + m + 1], wide)
                column = column - ratios[m] * element
            pivot = jnp.broadcast_to(column[at : at + 1], wide)
            if floor:
                least = jnp.maximum(floor * gram[at : at + 1, at : at + 1], 1e-37)
                pivot = jnp.maximum(pivot, least)
            ratios.append(jnp.where(row_at > at, column / pivot, 0.0))
            scales = jnp.where(row_at == at, lax.rsqrt(pivot), scales)
        for k in range(STEP):
            work = work - ratios[k] * jnp.broadcast_to(work[first + k : first + k + 1], wide)
    diagonal = jnp.where(rows == columns, 1.0 / scales[:, :VECS], 0.0)
    work = work * scales
    upper = jnp.where(rows < columns, work[:, :VECS], diagonal)
    return upper, work[:, VECS:]


def first_kernel(mine_ref, others_ref, *refs):
    others_ref, refs = (others_ref, *refs[: Y - 2]), refs[Y - 2 :]
    state_ref, scaled_ref, gram_ref, upper_ref, inputs_ref = refs
    drive = mine_ref[...]

    def gram_part(piece):
        return jnp.concatenate((piece[GRAM_ROW:, :128], piece[GRAM_ROW:, 128:256]))

    inputs_ref[lax.axis_index("y")] = gram_part(drive)
    for shift, other_ref in enumerate(others_ref, 1):
        other = other_ref[...]
        drive = drive + other
        inputs_ref[lax.rem(lax.axis_index("y") + (Y - shift), Y)] = gram_part(other)
    state = jnp.tanh(SCALE * drive[VECS : VECS + 1])
    grown = (SCALE * (1.0 - state * state)) * drive[:VECS]
    inputs = inputs_ref[0]
    for k in range(1, Y):
        inputs = inputs + inputs_ref[k]
    upper, inverse = factor(unpack_gram(inputs), 1e-6)
    scaled = dot(inverse, grown)
    state_ref[...] = state
    scaled_ref[...] = scaled
    gram_ref[...] = jnp.broadcast_to(pack_gram(gram_of(scaled)), gram_ref.shape)
    upper_ref[...] = upper


def second_kernel(grams_ref, scaled_ref, input_upper_ref, result_ref, product_ref, upper_ref):
    gram = unpack_gram(jnp.sum(grams_ref[...], axis=0))
    near_upper, inverse = factor(gram)
    first = dot(inverse, scaled_ref[...])
    upper = dot(near_upper, input_upper_ref[...])
    gram_two = lax.dot_general(
        dot(inverse, gram),
        inverse,
        (((1,), (1,)), ((), ())),
        precision=HIGH,
        preferred_element_type=jnp.float32,
    )
    second_upper, second_inverse = factor(gram_two)
    result_ref[...] = dot(second_inverse, first)
    product_ref[...] = dot(second_upper, upper)
    upper_ref[...] = upper


def gather_grams(copies):
    near = jnp.sum(lax.all_to_all(copies, ("x", "core", "y"), 0, 0), axis=0)
    return lax.all_to_all(jnp.broadcast_to(near, (Z, *near.shape)), "z", 0, 0)


def per_device(tangent, activity, block_keys):
    block = jax.ShapeDtypeStruct((PAD, OWN), jnp.bfloat16)
    own = pl.pallas_call(own_kernel, out_shape=block, compiler_params=PARAMS)(
        tangent, activity.reshape(OWN // 128, 128)
    )
    shards = [
        lax.ppermute(own, "x", [(i, (i + shift) % X) for i in range(X)]) for shift in range(1, X)
    ]
    start = pl.pallas_call(
        shard_kernel,
        in_specs=[SMEM, VMEM],
        out_shape=jax.ShapeDtypeStruct((PAD, ROWS), jnp.float32),
        scratch_shapes=[pltpu.VMEM((OWN // GROUP, 128), jnp.int32)],
        cost_estimate=pl.CostEstimate(
            flops=OWN * ROWS * 1500, bytes_accessed=PAD * OWN * 2, transcendentals=0
        ),
        compiler_params=PARAMS,
    )(block_keys, own)
    shards, start = lax.optimization_barrier((shards, start))
    mine = jnp.stack([own] + shards)
    others = lax.ppermute(mine, "core", [(0, 1), (1, 0)])
    near = pl.pallas_call(
        block_kernel,
        in_specs=[SMEM, VMEM, VMEM],
        out_shape=jax.ShapeDtypeStruct((PAD, SEG), jnp.bfloat16),
        compiler_params=PARAMS,
    )(block_keys, mine, others)

    up = [(i, (i + 1) % Z) for i in range(Z)]
    down = [(i, (i - 1) % Z) for i in range(Z)]
    below, above = lax.ppermute(near, "z", up), lax.ppermute(near, "z", down)
    earlier = partial_drive((0,), [near], (start,))
    for step in range(1, Z // 2):
        next_below = lax.ppermute(below, "z", up)
        next_above = lax.ppermute(above, "z", down) if step + 1 < Z // 2 else None
        unroll = 2 if step == 1 else 1
        earlier = partial_drive((-step, step), [below, above], earlier, unroll=unroll)
        below, above = next_below, next_above
    *sent, _ = partial_drive((Z // 2,), [below], earlier, tuple(range(1, Y)))
    kept, _ = partial_drive((Z // 2,), [below], earlier, (0,))
    pieces = [kept] + [
        lax.ppermute(piece, "y", [(i, (i + shift) % Y) for i in range(Y)])
        for shift, piece in enumerate(sent, 1)
    ]

    square = jax.ShapeDtypeStruct((VECS, VECS), jnp.float32)
    wide = jax.ShapeDtypeStruct((VECS, OWN), jnp.float32)
    state, scaled, gram, input_upper = pl.pallas_call(
        first_kernel,
        out_shape=(
            jax.ShapeDtypeStruct((1, OWN), jnp.float32),
            wide,
            jax.ShapeDtypeStruct((X * CORE * Y, 8, 128), jnp.float32),
            square,
        ),
        compiler_params=PARAMS,
        scratch_shapes=[pltpu.VMEM((Y, 8, 128), jnp.float32)],
    )(*pieces)
    result, product, upper = pl.pallas_call(
        second_kernel, out_shape=(wide, square, square), compiler_params=PARAMS
    )(gather_grams(gram), scaled, input_upper)
    return result, state.reshape(OWN), product, upper


def solution(mesh):
    split = Mesh(mesh.devices.reshape(X, CORE, Z, Y), ("x", "core", "z", "y"))
    columns, rows = ("z", "y", "x", "core"), ("x", "core", "z", "y")
    return jax.shard_map(
        per_device,
        mesh=split,
        in_specs=(P(None, columns), P(columns), P(("x", "core"), ("z", "y"))),
        out_specs=(P(None, rows), P(rows), P(), P()),
        check_vma=False,
    )
```

```python
import functools
import math

import jax
import jax.numpy as jnp
from jax import lax
from jax.experimental import pallas as pl
from jax.experimental.pallas import tpu as pltpu
from jax.sharding import Mesh
from jax.sharding import PartitionSpec as P

N = 131072
VECS = 32
PAD = 48
KEYCOLS = 256
X, CORE, Z, Y = 4, 2, 8, 4
OWN = N // (X * CORE * Z * Y)
ROWS = OWN * Y
SEG = OWN * X * CORE
GROUP = 32
SPARE = 40
SENT = 40
GRAM_ROW = 36
LANES = 512
KEYS = SEG // KEYCOLS
GRAM_TILE = 4 * (KEYS // 8)
SCALE = 2.0 / math.sqrt(5461.25 * N)
HIGH = lax.Precision.HIGHEST
PARAMS = pltpu.CompilerParams(vmem_limit_bytes=16 * 2**20)
STEP = 16
VMEM = pl.BlockSpec(memory_space=pltpu.VMEM)
SMEM = pl.BlockSpec(memory_space=pltpu.SMEM)


def shift_right(value, amount):
    return lax.shift_right_logical(value, jnp.full(value.shape, amount, jnp.int32))


def coupling(value):
    value = value ^ shift_right(value, 15)
    value = value * jnp.int32(739982445)
    value = value ^ shift_right(value, 13)
    value = value * jnp.int32(695872825)
    value = value ^ shift_right(value, 16)
    return (value.astype(jnp.int8) ^ jnp.int8(-128)).astype(jnp.bfloat16)


def spare_tile(block_ref, tile):
    return block_ref[SPARE - 8 : SPARE + 8, 128 * tile : 128 * tile + 128].astype(jnp.float32)[8:]


def own_kernel(tangent_ref, activity_ref, own_ref):
    parts = [activity_ref[k : k + 1, :].astype(jnp.float32) for k in range(OWN // 128)]
    rest = jnp.zeros((PAD - VECS - 1, OWN), jnp.float32)
    rest = jnp.concatenate((jnp.concatenate(parts, axis=1), rest))
    own_ref[:VECS, :] = tangent_ref[...]
    own_ref[VECS:, :] = rest.astype(jnp.bfloat16)


def block_kernel(keys_ref, mine_ref, others_ref, block_ref):
    shards_refs = (mine_ref, others_ref)
    for core in range(CORE):
        at = jnp.bitwise_xor(lax.axis_index("core"), core) * OWN
        for shift in range(X):
            chip = lax.rem(lax.axis_index("x") + (X - shift), X)
            lanes = pl.ds(pl.multiple_of(chip * (CORE * OWN) + at, OWN), OWN)
            block_ref[:, lanes] = shards_refs[core][shift]
    own = block_ref[:VECS, :]
    gram = lax.dot_general(own, own, (((1,), (1,)), ((), ())), preferred_element_type=jnp.float32)
    rest = pack_gram(gram / N)
    rows = lax.broadcasted_iota(jnp.int32, (8, 128), 0)
    parts = []
    for part in range(KEYS // 8):
        keys = jnp.zeros((8, 128), jnp.int32)
        for row in range(8):
            keys = jnp.where(rows == row, keys_ref[0, part * 8 + row], keys)
        parts.append(keys)
    tiles = []
    for digit in range(4):
        for keys in parts:
            tiles.append(jnp.bitwise_and(shift_right(keys, 8 * digit), 255).astype(jnp.float32))
    for _ in range(3):
        part = rest.astype(jnp.bfloat16).astype(jnp.float32)
        tiles.append(part)
        rest = rest - part
    for k, tile in enumerate(tiles):
        lanes = slice(128 * k, 128 * k + 128)
        above = block_ref[SPARE - 8 : SPARE + 8, lanes].astype(jnp.float32)[:8]
        block_ref[SPARE - 8 : SPARE + 8, lanes] = jnp.concatenate((above, tile)).astype(jnp.bfloat16)


def shard_index():
    return lax.axis_index("x") * CORE + lax.axis_index("core")


def row_starts(lane):
    first_row = shard_index() * (N // (X * CORE)) + lax.axis_index("z") * ROWS + lane
    row_at = lax.broadcasted_iota(jnp.int32, (GROUP, 128), 1)
    spread = lax.broadcasted_iota(jnp.int32, (GROUP, 128), 0) * jnp.int32(668265261)
    return [
        (first_row + 128 * k + row_at) * jnp.int32(374761393) + spread
        for k in range(LANES // 128)
    ]


def product(vectors, bases, starts):
    parts = [
        jnp.concatenate([coupling(base + start) for start in starts], axis=1) for base in bases
    ]
    return jnp.dot(
        vectors, jnp.concatenate(parts, axis=0), preferred_element_type=jnp.float32
    )


def shard_kernel(keys_ref, own_ref, out_ref, bases_ref):
    shard = shard_index()
    place = lax.axis_index("z") * Y + lax.axis_index("y")
    steps = lax.broadcasted_iota(jnp.int32, (8, 128), 0) * jnp.int32(GROUP)
    for k in range(OWN // KEYCOLS):
        key = keys_ref[0, shard * (OWN // KEYCOLS) + k]
        columns = place * SEG + shard * OWN + k * KEYCOLS + steps
        bases_ref[8 * k : 8 * k + 8, :] = key + columns * jnp.int32(668265261)

    def lanes_body(number, carry):
        lane = pl.multiple_of(number * LANES, LANES)
        bases = [bases_ref[k : k + 1, :] for k in range(OWN // GROUP)]
        out_ref[:, pl.ds(lane, LANES)] = product(own_ref[...], bases, row_starts(lane))
        return carry

    lax.fori_loop(0, Y, lanes_body, 0)


def drive_kernel(*refs, shifts, earlier, parts, pieces, unroll):
    blocks = len(shifts)
    block_refs = refs[:blocks]
    earlier_refs = refs[blocks : blocks + earlier]
    *out_refs, grams_ref, total_ref, vectors_ref, bases_ref = refs[blocks + earlier :]
    groups = SEG // GROUP

    for slot in range(Z):
        grams_ref[slot] = earlier_refs[1][slot] if earlier == 2 else jnp.zeros((8, 128), jnp.float32)
    steps = lax.broadcasted_iota(jnp.int32, (8, 128), 0) * jnp.int32(GROUP)
    for k, shift in enumerate(shifts):
        place = lax.rem(lax.axis_index("z") + (Z + shift), Z)
        vectors_ref[k] = block_refs[k][...]
        gram = jnp.zeros((8, 128), jnp.float32)
        for part in range(3):
            gram = gram + spare_tile(block_refs[k], GRAM_TILE + part)
        grams_ref[place] = gram
        first_column = (place * Y + lax.axis_index("y")) * SEG
        for part in range(KEYS // 8):
            keys = jnp.zeros((8, 128), jnp.int32)
            for digit in range(4):
                tile = spare_tile(block_refs[k], digit * (KEYS // 8) + part)
                keys = keys + tile.astype(jnp.int32) * jnp.int32(256**digit)
            for row in range(8):
                key = part * 8 + row
                columns = first_column + key * KEYCOLS + steps
                at = k * groups + key * 8
                bases_ref[at : at + 8, :] = keys[row : row + 1] + columns * jnp.int32(668265261)

    def part_at(number):
        return lax.rem(lax.axis_index("y") + (parts[0] + number), Y) if parts else number

    def step_body(step, carry):
        if len(parts) == 1:
            number, block = 0, step
        else:
            number = lax.shift_right_logical(step, blocks - 1)
            block = jnp.bitwise_and(step, blocks - 1)
        lane = pl.multiple_of(part_at(number) * LANES, LANES)
        here = pl.ds(lane, LANES)
        if earlier == 1:
            shards = [
                jnp.bitwise_and(shard_index() + shift, X * CORE - 1) for shift in range(1, X * CORE)
            ]
            bases = []
            vectors = []
            for shard in shards:
                first = pl.multiple_of(shard * (OWN // GROUP), OWN // GROUP)
                bases += [bases_ref[pl.ds(first + k, 1), :] for k in range(OWN // GROUP)]
                vectors.append(vectors_ref[0, :, pl.ds(pl.multiple_of(shard * OWN, OWN), OWN)])
            vectors = jnp.concatenate(vectors, axis=1)
        else:
            first = pl.multiple_of(block * groups, groups)
            bases = [bases_ref[pl.ds(first + group, 1), :] for group in range(groups)]
            vectors = vectors_ref[block]
        total_ref[:, here] += product(vectors, bases, row_starts(lane))
        return carry

    total_ref[...] = earlier_refs[0][...]
    lax.fori_loop(0, (len(parts) or Y) * blocks, step_body, 0, unroll=unroll)
    if not pieces:
        out_refs[0][...] = total_ref[...]
        return
    gram = grams_ref[0]
    for slot in range(1, Z):
        gram = gram + grams_ref[slot]
    for number, out_ref in enumerate(out_refs):
        lane = pl.multiple_of(part_at(number) * LANES, LANES)
        out_ref[...] = total_ref[:SENT, pl.ds(lane, LANES)]
        out_ref[GRAM_ROW:, :128] = gram[:4]
        out_ref[GRAM_ROW:, 128:256] = gram[4:]


def partial_drive(shifts, blocks, earlier=(), parts=(), pieces=False, unroll=1):
    count = len(blocks)
    drive = jax.ShapeDtypeStruct((PAD, ROWS), jnp.float32)
    if pieces:
        out_shape = [jax.ShapeDtypeStruct((SENT, OWN), jnp.float32)] * len(parts)
    else:
        out_shape = [drive]
    grams = jax.ShapeDtypeStruct((Z, 8, 128), jnp.float32)
    return pl.pallas_call(
        functools.partial(
            drive_kernel,
            shifts=shifts,
            earlier=len(earlier),
            parts=parts,
            pieces=pieces,
            unroll=unroll,
        ),
        in_specs=[VMEM] * (count + len(earlier)),
        out_specs=[VMEM] * (len(out_shape) + 1),
        out_shape=out_shape + [grams],
        scratch_shapes=[
            pltpu.VMEM(drive.shape, jnp.float32),
            pltpu.VMEM((count, PAD, SEG), jnp.bfloat16),
            pltpu.VMEM((count * SEG // GROUP, 128), jnp.int32),
        ],
        cost_estimate=pl.CostEstimate(
            flops=count * SEG * (len(parts) or Y) * LANES * 1500,
            bytes_accessed=count * PAD * SEG * 2,
            transcendentals=0,
        ),
        compiler_params=PARAMS,
    )(*blocks, *earlier)


def pack_gram(gram):
    return jnp.concatenate([gram[8 * k : 8 * k + 8] for k in range(4)], axis=1)


def unpack_gram(packed):
    return jnp.concatenate([packed[:, 32 * k : 32 * k + 32] for k in range(4)], axis=0)


def gram_of(rows):
    return lax.dot_general(
        rows, rows, (((1,), (1,)), ((), ())), precision=HIGH, preferred_element_type=jnp.float32
    ) / N


def dot(left, right):
    return jnp.dot(left, right, precision=HIGH, preferred_element_type=jnp.float32)


def factor(gram, floor=0.0):
    rows = lax.broadcasted_iota(jnp.int32, (VECS, VECS), 0)
    columns = lax.broadcasted_iota(jnp.int32, (VECS, VECS), 1)
    wide = (VECS, 2 * VECS)
    row_at = lax.broadcasted_iota(jnp.int32, wide, 0)
    work = jnp.concatenate((gram, (rows == columns).astype(jnp.float32)), axis=1)
    scales = jnp.zeros(wide, jnp.float32)
    for first in range(0, VECS, STEP):
        spread = [
            jnp.broadcast_to(work[:, first + k : first + k + 1], wide) for k in range(STEP)
        ]
        ratios = []
        for k in range(STEP):
            at = first + k
            column = spread[k]
            for m in range(k):
                element = jnp.broadcast_to(column[first + m : first + m + 1], wide)
                column = column - ratios[m] * element
            pivot = jnp.broadcast_to(column[at : at + 1], wide)
            if floor:
                least = jnp.maximum(floor * gram[at : at + 1, at : at + 1], 1e-37)
                pivot = jnp.maximum(pivot, least)
            ratios.append(jnp.where(row_at > at, column / pivot, 0.0))
            scales = jnp.where(row_at == at, lax.rsqrt(pivot), scales)
        for k in range(STEP):
            work = work - ratios[k] * jnp.broadcast_to(work[first + k : first + k + 1], wide)
    diagonal = jnp.where(rows == columns, 1.0 / scales[:, :VECS], 0.0)
    work = work * scales
    upper = jnp.where(rows < columns, work[:, :VECS], diagonal)
    return upper, work[:, VECS:]


def first_kernel(mine_ref, others_ref, *refs):
    others_ref, refs = (others_ref, *refs[: Y - 2]), refs[Y - 2 :]
    state_ref, scaled_ref, gram_ref, upper_ref, inputs_ref = refs
    drive = mine_ref[...]

    def gram_part(piece):
        return jnp.concatenate((piece[GRAM_ROW:, :128], piece[GRAM_ROW:, 128:256]))

    inputs_ref[lax.axis_index("y")] = gram_part(drive)
    for shift, other_ref in enumerate(others_ref, 1):
        other = other_ref[...]
        drive = drive + other
        inputs_ref[lax.rem(lax.axis_index("y") + (Y - shift), Y)] = gram_part(other)
    state = jnp.tanh(SCALE * drive[VECS : VECS + 1])
    grown = (SCALE * (1.0 - state * state)) * drive[:VECS]
    inputs = inputs_ref[0]
    for k in range(1, Y):
        inputs = inputs + inputs_ref[k]
    upper, inverse = factor(unpack_gram(inputs), 1e-6)
    scaled = dot(inverse, grown)
    state_ref[...] = state
    scaled_ref[...] = scaled
    gram_ref[...] = jnp.broadcast_to(pack_gram(gram_of(scaled)), gram_ref.shape)
    upper_ref[...] = upper


def second_kernel(grams_ref, scaled_ref, input_upper_ref, result_ref, product_ref, upper_ref):
    gram = unpack_gram(jnp.sum(grams_ref[...], axis=0))
    near_upper, inverse = factor(gram)
    first = dot(inverse, scaled_ref[...])
    upper = dot(near_upper, input_upper_ref[...])
    gram_two = lax.dot_general(
        dot(inverse, gram),
        inverse,
        (((1,), (1,)), ((), ())),
        precision=HIGH,
        preferred_element_type=jnp.float32,
    )
    second_upper, second_inverse = factor(gram_two)
    result_ref[...] = dot(second_inverse, first)
    product_ref[...] = dot(second_upper, upper)
    upper_ref[...] = upper


def gather_grams(copies):
    near = jnp.sum(lax.all_to_all(copies, ("x", "core", "y"), 0, 0), axis=0)
    return lax.all_to_all(jnp.broadcast_to(near, (Z, *near.shape)), "z", 0, 0)


def per_device(tangent, activity, block_keys):
    block = jax.ShapeDtypeStruct((PAD, OWN), jnp.bfloat16)
    own = pl.pallas_call(own_kernel, out_shape=block, compiler_params=PARAMS)(
        tangent, activity.reshape(OWN // 128, 128)
    )
    shards = [
        lax.ppermute(own, "x", [(i, (i + shift) % X) for i in range(X)]) for shift in range(1, X)
    ]
    start = pl.pallas_call(
        shard_kernel,
        in_specs=[SMEM, VMEM],
        out_shape=jax.ShapeDtypeStruct((PAD, ROWS), jnp.float32),
        scratch_shapes=[pltpu.VMEM((OWN // GROUP, 128), jnp.int32)],
        cost_estimate=pl.CostEstimate(
            flops=OWN * ROWS * 1500, bytes_accessed=PAD * OWN * 2, transcendentals=0
        ),
        compiler_params=PARAMS,
    )(block_keys, own)
    shards, start = lax.optimization_barrier((shards, start))
    mine = jnp.stack([own] + shards)
    others = lax.ppermute(mine, "core", [(0, 1), (1, 0)])
    near = pl.pallas_call(
        block_kernel,
        in_specs=[SMEM, VMEM, VMEM],
        out_shape=jax.ShapeDtypeStruct((PAD, SEG), jnp.bfloat16),
        compiler_params=PARAMS,
    )(block_keys, mine, others)

    up = [(i, (i + 1) % Z) for i in range(Z)]
    down = [(i, (i - 1) % Z) for i in range(Z)]
    below, above = lax.ppermute(near, "z", up), lax.ppermute(near, "z", down)
    earlier = partial_drive((0,), [near], (start,))
    for step in range(1, Z // 2):
        next_below = lax.ppermute(below, "z", up)
        next_above = lax.ppermute(above, "z", down) if step + 1 < Z // 2 else None
        unroll = 2 if step == 1 else 1
        parts = tuple(range(1, Y)) if step + 1 == Z // 2 else ()
        earlier = partial_drive((-step, step), [below, above], earlier, parts, unroll=unroll)
        last = [below, above]
        below, above = next_below, next_above
    *sent, _ = partial_drive((Z // 2,), [below], earlier, tuple(range(1, Y)), pieces=True)
    shifts = (1 - Z // 2, Z // 2 - 1, Z // 2)
    kept, _ = partial_drive(shifts, last + [below], earlier, (0,), pieces=True)
    pieces = [kept] + [
        lax.ppermute(piece, "y", [(i, (i + shift) % Y) for i in range(Y)])
        for shift, piece in enumerate(sent, 1)
    ]

    square = jax.ShapeDtypeStruct((VECS, VECS), jnp.float32)
    wide = jax.ShapeDtypeStruct((VECS, OWN), jnp.float32)
    state, scaled, gram, input_upper = pl.pallas_call(
        first_kernel,
        out_shape=(
            jax.ShapeDtypeStruct((1, OWN), jnp.float32),
            wide,
            jax.ShapeDtypeStruct((X * CORE * Y, 8, 128), jnp.float32),
            square,
        ),
        compiler_params=PARAMS,
        scratch_shapes=[pltpu.VMEM((Y, 8, 128), jnp.float32)],
    )(*pieces)
    result, product, upper = pl.pallas_call(
        second_kernel, out_shape=(wide, square, square), compiler_params=PARAMS
    )(gather_grams(gram), scaled, input_upper)
    return result, state.reshape(OWN), product, upper


def solution(mesh):
    split = Mesh(mesh.devices.reshape(X, CORE, Z, Y), ("x", "core", "z", "y"))
    columns, rows = ("z", "y", "x", "core"), ("x", "core", "z", "y")
    return jax.shard_map(
        per_device,
        mesh=split,
        in_specs=(P(None, columns), P(columns), P(("x", "core"), ("z", "y"))),
        out_specs=(P(None, rows), P(rows), P(), P()),
        check_vma=False,
    )
```

```python
import functools
import math

import jax
import jax.numpy as jnp
from jax import lax
from jax.experimental import pallas as pl
from jax.experimental.pallas import tpu as pltpu
from jax.sharding import Mesh
from jax.sharding import PartitionSpec as P

N = 131072
VECS = 32
PAD = 48
KEYCOLS = 256
X, CORE, Z, Y = 4, 2, 8, 4
OWN = N // (X * CORE * Z * Y)
ROWS = OWN * Y
SEG = OWN * X * CORE
GROUP = 32
SPARE = 40
FROM = (0, 2, 1, 3)
SENT = 40
GRAM_ROW = 36
LANES = 512
KEYS = SEG // KEYCOLS
GRAM_TILE = 4 * (KEYS // 8)
SCALE = 2.0 / math.sqrt(5461.25 * N)
HIGH = lax.Precision.HIGHEST
PARAMS = pltpu.CompilerParams(vmem_limit_bytes=16 * 2**20)
STEP = 16
VMEM = pl.BlockSpec(memory_space=pltpu.VMEM)
SMEM = pl.BlockSpec(memory_space=pltpu.SMEM)


def shift_right(value, amount):
    return lax.shift_right_logical(value, jnp.full(value.shape, amount, jnp.int32))


def coupling(value):
    value = value ^ shift_right(value, 15)
    value = value * jnp.int32(739982445)
    value = value ^ shift_right(value, 13)
    value = value * jnp.int32(695872825)
    value = value ^ shift_right(value, 16)
    return (value.astype(jnp.int8) ^ jnp.int8(-128)).astype(jnp.bfloat16)


def spare_tile(block_ref, tile):
    return block_ref[SPARE - 8 : SPARE + 8, 128 * tile : 128 * tile + 128].astype(jnp.float32)[8:]


def own_kernel(tangent_ref, activity_ref, own_ref):
    parts = [activity_ref[k : k + 1, :].astype(jnp.float32) for k in range(OWN // 128)]
    rest = jnp.zeros((PAD - VECS - 1, OWN), jnp.float32)
    rest = jnp.concatenate((jnp.concatenate(parts, axis=1), rest))
    own_ref[:VECS, :] = tangent_ref[...]
    own_ref[VECS:, :] = rest.astype(jnp.bfloat16)


def block_kernel(keys_ref, mine_ref, others_ref, block_ref):
    shards_refs = (mine_ref, others_ref)
    for core in range(CORE):
        at = jnp.bitwise_xor(lax.axis_index("core"), core) * OWN
        for slot, shift in enumerate(FROM):
            chip = lax.rem(lax.axis_index("x") + (X - shift), X)
            lanes = pl.ds(pl.multiple_of(chip * (CORE * OWN) + at, OWN), OWN)
            block_ref[:, lanes] = shards_refs[core][slot]
    own = block_ref[:VECS, :]
    gram = lax.dot_general(own, own, (((1,), (1,)), ((), ())), preferred_element_type=jnp.float32)
    rest = pack_gram(gram / N)
    rows = lax.broadcasted_iota(jnp.int32, (8, 128), 0)
    parts = []
    for part in range(KEYS // 8):
        keys = jnp.zeros((8, 128), jnp.int32)
        for row in range(8):
            keys = jnp.where(rows == row, keys_ref[0, part * 8 + row], keys)
        parts.append(keys)
    tiles = []
    for digit in range(4):
        for keys in parts:
            tiles.append(jnp.bitwise_and(shift_right(keys, 8 * digit), 255).astype(jnp.float32))
    for _ in range(3):
        part = rest.astype(jnp.bfloat16).astype(jnp.float32)
        tiles.append(part)
        rest = rest - part
    for k, tile in enumerate(tiles):
        lanes = slice(128 * k, 128 * k + 128)
        above = block_ref[SPARE - 8 : SPARE + 8, lanes].astype(jnp.float32)[:8]
        block_ref[SPARE - 8 : SPARE + 8, lanes] = jnp.concatenate((above, tile)).astype(jnp.bfloat16)


def shard_index():
    return lax.axis_index("x") * CORE + lax.axis_index("core")


def row_starts(lane):
    first_row = shard_index() * (N // (X * CORE)) + lax.axis_index("z") * ROWS + lane
    row_at = lax.broadcasted_iota(jnp.int32, (GROUP, 128), 1)
    spread = lax.broadcasted_iota(jnp.int32, (GROUP, 128), 0) * jnp.int32(668265261)
    return [
        (first_row + 128 * k + row_at) * jnp.int32(374761393) + spread
        for k in range(LANES // 128)
    ]


def product(vectors, bases, starts):
    parts = [
        jnp.concatenate([coupling(base + start) for start in starts], axis=1) for base in bases
    ]
    return jnp.dot(
        vectors, jnp.concatenate(parts, axis=0), preferred_element_type=jnp.float32
    )


def shard_kernel(keys_ref, own_ref, out_ref, bases_ref):
    shard = shard_index()
    place = lax.axis_index("z") * Y + lax.axis_index("y")
    steps = lax.broadcasted_iota(jnp.int32, (8, 128), 0) * jnp.int32(GROUP)
    for k in range(OWN // KEYCOLS):
        key = keys_ref[0, shard * (OWN // KEYCOLS) + k]
        columns = place * SEG + shard * OWN + k * KEYCOLS + steps
        bases_ref[8 * k : 8 * k + 8, :] = key + columns * jnp.int32(668265261)

    def lanes_body(number, carry):
        lane = pl.multiple_of(number * LANES, LANES)
        bases = [bases_ref[k : k + 1, :] for k in range(OWN // GROUP)]
        out_ref[:, pl.ds(lane, LANES)] = product(own_ref[...], bases, row_starts(lane))
        return carry

    lax.fori_loop(0, Y, lanes_body, 0)


def drive_kernel(*refs, shifts, earlier, parts, pieces, unroll):
    blocks = len(shifts)
    block_refs = refs[:blocks]
    earlier_refs = refs[blocks : blocks + earlier]
    *out_refs, grams_ref, total_ref, vectors_ref, bases_ref = refs[blocks + earlier :]
    groups = SEG // GROUP

    for slot in range(Z):
        grams_ref[slot] = earlier_refs[1][slot] if earlier == 2 else jnp.zeros((8, 128), jnp.float32)
    steps = lax.broadcasted_iota(jnp.int32, (8, 128), 0) * jnp.int32(GROUP)
    for k, shift in enumerate(shifts):
        place = lax.rem(lax.axis_index("z") + (Z + shift), Z)
        vectors_ref[k] = block_refs[k][...]
        gram = jnp.zeros((8, 128), jnp.float32)
        for part in range(3):
            gram = gram + spare_tile(block_refs[k], GRAM_TILE + part)
        grams_ref[place] = gram
        first_column = (place * Y + lax.axis_index("y")) * SEG
        for part in range(KEYS // 8):
            keys = jnp.zeros((8, 128), jnp.int32)
            for digit in range(4):
                tile = spare_tile(block_refs[k], digit * (KEYS // 8) + part)
                keys = keys + tile.astype(jnp.int32) * jnp.int32(256**digit)
            for row in range(8):
                key = part * 8 + row
                columns = first_column + key * KEYCOLS + steps
                at = k * groups + key * 8
                bases_ref[at : at + 8, :] = keys[row : row + 1] + columns * jnp.int32(668265261)

    def part_at(number):
        return lax.rem(lax.axis_index("y") + (parts[0] + number), Y) if parts else number

    def step_body(step, carry):
        if len(parts) == 1:
            number, block = 0, step
        else:
            number = lax.shift_right_logical(step, blocks - 1)
            block = jnp.bitwise_and(step, blocks - 1)
        lane = pl.multiple_of(part_at(number) * LANES, LANES)
        here = pl.ds(lane, LANES)
        if earlier == 1:
            shards = [
                jnp.bitwise_and(shard_index() + shift, X * CORE - 1) for shift in range(1, X * CORE)
            ]
            bases = []
            vectors = []
            for shard in shards:
                first = pl.multiple_of(shard * (OWN // GROUP), OWN // GROUP)
                bases += [bases_ref[pl.ds(first + k, 1), :] for k in range(OWN // GROUP)]
                vectors.append(vectors_ref[0, :, pl.ds(pl.multiple_of(shard * OWN, OWN), OWN)])
            vectors = jnp.concatenate(vectors, axis=1)
        else:
            first = pl.multiple_of(block * groups, groups)
            bases = [bases_ref[pl.ds(first + group, 1), :] for group in range(groups)]
            vectors = vectors_ref[block]
        total_ref[:, here] += product(vectors, bases, row_starts(lane))
        return carry

    total_ref[...] = earlier_refs[0][...]
    lax.fori_loop(0, (len(parts) or Y) * blocks, step_body, 0, unroll=unroll)
    if not pieces:
        out_refs[0][...] = total_ref[...]
        return
    gram = grams_ref[0]
    for slot in range(1, Z):
        gram = gram + grams_ref[slot]
    for number, out_ref in enumerate(out_refs):
        lane = pl.multiple_of(part_at(number) * LANES, LANES)
        out_ref[...] = total_ref[:SENT, pl.ds(lane, LANES)]
        out_ref[GRAM_ROW:, :128] = gram[:4]
        out_ref[GRAM_ROW:, 128:256] = gram[4:]


def partial_drive(shifts, blocks, earlier=(), parts=(), pieces=False, unroll=1):
    count = len(blocks)
    drive = jax.ShapeDtypeStruct((PAD, ROWS), jnp.float32)
    if pieces:
        out_shape = [jax.ShapeDtypeStruct((SENT, OWN), jnp.float32)] * len(parts)
    else:
        out_shape = [drive]
    grams = jax.ShapeDtypeStruct((Z, 8, 128), jnp.float32)
    return pl.pallas_call(
        functools.partial(
            drive_kernel,
            shifts=shifts,
            earlier=len(earlier),
            parts=parts,
            pieces=pieces,
            unroll=unroll,
        ),
        in_specs=[VMEM] * (count + len(earlier)),
        out_specs=[VMEM] * (len(out_shape) + 1),
        out_shape=out_shape + [grams],
        scratch_shapes=[
            pltpu.VMEM(drive.shape, jnp.float32),
            pltpu.VMEM((count, PAD, SEG), jnp.bfloat16),
            pltpu.VMEM((count * SEG // GROUP, 128), jnp.int32),
        ],
        cost_estimate=pl.CostEstimate(
            flops=count * SEG * (len(parts) or Y) * LANES * 1500,
            bytes_accessed=count * PAD * SEG * 2,
            transcendentals=0,
        ),
        compiler_params=PARAMS,
    )(*blocks, *earlier)


def pack_gram(gram):
    return jnp.concatenate([gram[8 * k : 8 * k + 8] for k in range(4)], axis=1)


def unpack_gram(packed):
    return jnp.concatenate([packed[:, 32 * k : 32 * k + 32] for k in range(4)], axis=0)


def gram_of(rows):
    return lax.dot_general(
        rows, rows, (((1,), (1,)), ((), ())), precision=HIGH, preferred_element_type=jnp.float32
    ) / N


def dot(left, right):
    return jnp.dot(left, right, precision=HIGH, preferred_element_type=jnp.float32)


def factor(gram, floor=0.0):
    rows = lax.broadcasted_iota(jnp.int32, (VECS, VECS), 0)
    columns = lax.broadcasted_iota(jnp.int32, (VECS, VECS), 1)
    wide = (VECS, 2 * VECS)
    row_at = lax.broadcasted_iota(jnp.int32, wide, 0)
    work = jnp.concatenate((gram, (rows == columns).astype(jnp.float32)), axis=1)
    scales = jnp.zeros(wide, jnp.float32)
    for first in range(0, VECS, STEP):
        spread = [
            jnp.broadcast_to(work[:, first + k : first + k + 1], wide) for k in range(STEP)
        ]
        ratios = []
        for k in range(STEP):
            at = first + k
            column = spread[k]
            for m in range(k):
                element = jnp.broadcast_to(column[first + m : first + m + 1], wide)
                column = column - ratios[m] * element
            pivot = jnp.broadcast_to(column[at : at + 1], wide)
            if floor:
                least = jnp.maximum(floor * gram[at : at + 1, at : at + 1], 1e-37)
                pivot = jnp.maximum(pivot, least)
            ratios.append(jnp.where(row_at > at, column / pivot, 0.0))
            scales = jnp.where(row_at == at, lax.rsqrt(pivot), scales)
        for k in range(STEP):
            work = work - ratios[k] * jnp.broadcast_to(work[first + k : first + k + 1], wide)
    diagonal = jnp.where(rows == columns, 1.0 / scales[:, :VECS], 0.0)
    work = work * scales
    upper = jnp.where(rows < columns, work[:, :VECS], diagonal)
    return upper, work[:, VECS:]


def first_kernel(mine_ref, others_ref, *refs):
    others_ref, refs = (others_ref, *refs[: Y - 2]), refs[Y - 2 :]
    state_ref, scaled_ref, gram_ref, upper_ref, inputs_ref = refs
    drive = mine_ref[...]

    def gram_part(piece):
        return jnp.concatenate((piece[GRAM_ROW:, :128], piece[GRAM_ROW:, 128:256]))

    inputs_ref[lax.axis_index("y")] = gram_part(drive)
    for shift, other_ref in enumerate(others_ref, 1):
        other = other_ref[...]
        drive = drive + other
        inputs_ref[lax.rem(lax.axis_index("y") + (Y - shift), Y)] = gram_part(other)
    state = jnp.tanh(SCALE * drive[VECS : VECS + 1])
    grown = (SCALE * (1.0 - state * state)) * drive[:VECS]
    inputs = inputs_ref[0]
    for k in range(1, Y):
        inputs = inputs + inputs_ref[k]
    upper, inverse = factor(unpack_gram(inputs), 1e-6)
    scaled = dot(inverse, grown)
    state_ref[...] = state
    scaled_ref[...] = scaled
    gram_ref[...] = jnp.broadcast_to(pack_gram(gram_of(scaled)), gram_ref.shape)
    upper_ref[...] = upper


def second_kernel(grams_ref, scaled_ref, input_upper_ref, result_ref, product_ref, upper_ref):
    gram = unpack_gram(jnp.sum(grams_ref[...], axis=0))
    near_upper, inverse = factor(gram)
    first = dot(inverse, scaled_ref[...])
    upper = dot(near_upper, input_upper_ref[...])
    gram_two = lax.dot_general(
        dot(inverse, gram),
        inverse,
        (((1,), (1,)), ((), ())),
        precision=HIGH,
        preferred_element_type=jnp.float32,
    )
    second_upper, second_inverse = factor(gram_two)
    result_ref[...] = dot(second_inverse, first)
    product_ref[...] = dot(second_upper, upper)
    upper_ref[...] = upper


def gather_grams(copies):
    near = jnp.sum(lax.all_to_all(copies, ("x", "core", "y"), 0, 0), axis=0)
    return lax.all_to_all(jnp.broadcast_to(near, (Z, *near.shape)), "z", 0, 0)


def per_device(tangent, activity, block_keys):
    block = jax.ShapeDtypeStruct((PAD, OWN), jnp.bfloat16)
    own = pl.pallas_call(own_kernel, out_shape=block, compiler_params=PARAMS)(
        tangent, activity.reshape(OWN // 128, 128)
    )
    shards = [
        lax.ppermute(own, "x", [(i, (i + shift) % X) for i in range(X)]) for shift in FROM[1:]
    ]
    start = pl.pallas_call(
        shard_kernel,
        in_specs=[SMEM, VMEM],
        out_shape=jax.ShapeDtypeStruct((PAD, ROWS), jnp.float32),
        scratch_shapes=[pltpu.VMEM((OWN // GROUP, 128), jnp.int32)],
        cost_estimate=pl.CostEstimate(
            flops=OWN * ROWS * 1500, bytes_accessed=PAD * OWN * 2, transcendentals=0
        ),
        compiler_params=PARAMS,
    )(block_keys, own)
    shards, start = lax.optimization_barrier((shards, start))
    mine = jnp.stack([own] + shards)
    others = lax.ppermute(mine, "core", [(0, 1), (1, 0)])
    near = pl.pallas_call(
        block_kernel,
        in_specs=[SMEM, VMEM, VMEM],
        out_shape=jax.ShapeDtypeStruct((PAD, SEG), jnp.bfloat16),
        compiler_params=PARAMS,
    )(block_keys, mine, others)

    up = [(i, (i + 1) % Z) for i in range(Z)]
    down = [(i, (i - 1) % Z) for i in range(Z)]
    below, above = lax.ppermute(near, "z", up), lax.ppermute(near, "z", down)
    earlier = partial_drive((0,), [near], (start,))
    for step in range(1, Z // 2):
        next_below = lax.ppermute(below, "z", up)
        next_above = lax.ppermute(above, "z", down) if step + 1 < Z // 2 else None
        unroll = 2 if step == 1 else 1
        parts = tuple(range(1, Y)) if step + 1 == Z // 2 else ()
        earlier = partial_drive((-step, step), [below, above], earlier, parts, unroll=unroll)
        last = [below, above]
        below, above = next_below, next_above
    *sent, _ = partial_drive((Z // 2,), [below], earlier, tuple(range(1, Y)), pieces=True)
    shifts = (1 - Z // 2, Z // 2 - 1, Z // 2)
    kept, _ = partial_drive(shifts, last + [below], earlier, (0,), pieces=True)
    pieces = [kept] + [
        lax.ppermute(piece, "y", [(i, (i + shift) % Y) for i in range(Y)])
        for shift, piece in enumerate(sent, 1)
    ]

    square = jax.ShapeDtypeStruct((VECS, VECS), jnp.float32)
    wide = jax.ShapeDtypeStruct((VECS, OWN), jnp.float32)
    state, scaled, gram, input_upper = pl.pallas_call(
        first_kernel,
        out_shape=(
            jax.ShapeDtypeStruct((1, OWN), jnp.float32),
            wide,
            jax.ShapeDtypeStruct((X * CORE * Y, 8, 128), jnp.float32),
            square,
        ),
        compiler_params=PARAMS,
        scratch_shapes=[pltpu.VMEM((Y, 8, 128), jnp.float32)],
    )(*pieces)
    result, product, upper = pl.pallas_call(
        second_kernel, out_shape=(wide, square, square), compiler_params=PARAMS
    )(gather_grams(gram), scaled, input_upper)
    return result, state.reshape(OWN), product, upper


def solution(mesh):
    split = Mesh(mesh.devices.reshape(X, CORE, Z, Y), ("x", "core", "z", "y"))
    columns, rows = ("z", "y", "x", "core"), ("x", "core", "z", "y")
    return jax.shard_map(
        per_device,
        mesh=split,
        in_specs=(P(None, columns), P(columns), P(("x", "core"), ("z", "y"))),
        out_specs=(P(None, rows), P(rows), P(), P()),
        check_vma=False,
    )
```
